32 devices in a mesh: groups: 2 (over y), dev: 8 (over z, x), tp: 2 (over core).
Axes of the slice: x: 2, y: 2, z: 4, core: 2. Of those that a mesh axis runs over, the one named last changes fastest.
Arguments:
- residual: bfloat16 [2048, 1024], P(('groups', 'dev'), 'tp'), parts along dimension 0, may hold values from -6 to 6
- queries: bfloat16 [2048, 1024], P(('groups', 'dev'), 'tp'), parts along dimension 0, may hold values from -8 to 8
- keys: bfloat16 [2048, 1024], P(('groups', 'dev'), 'tp'), parts along dimension 0, may hold values from -8 to 8
- values: bfloat16 [2048, 1024], P(('groups', 'dev'), 'tp'), parts along dimension 0, may hold values from -6 to 6
- tile_lists: int32 [64, 3], P(('groups', 'dev')), parts along dimension 0, may hold values from 0 to 3, as said below
- node_counts: int32 [16, 4], P(('groups', 'dev')), parts along dimension 0, may hold values from 1 to 64, 128 in all within a row
- norm_gain: float32 [1024], P('tp'), may hold values from 0.5 to 1.5
- expert_ids: int32 [2048, 2], P(('groups', 'dev')), parts along dimension 0, may hold values from 0 to 3, all different within a row; in each aligned block of 128 rows (0 to 127, 128 to 255, ...) at most 128 rows name the same one
- gate_codes: int32 [2048, 2], P(('groups', 'dev')), parts along dimension 0, may hold values from 8192 to 57344
- up_weight: bfloat16 [8, 1024, 2048], P('dev', None, 'tp'), may hold values from -0.1875 to 0.1875
- down_weight: bfloat16 [8, 2048, 1024], P('dev', 'tp'), may hold values from -0.09375 to 0.09375
Outputs:
- mixed: bfloat16 [2048, 1024], P(('groups', 'dev'), 'tp'), parts along dimension 0
The draws below stay inside these ranges and needn't reach their ends.
There are 2 independent parts, one for each index of `groups`. The reference program is written for one: setup_inputs(seed, part) draws one part's arguments, and reference() takes and returns one part's arrays. A program takes and returns all parts, laid end to end along the dimension named above; an argument that names none is the same for every part. Nothing has to cross between parts.
Inputs may be any that keep to these rules, and one draw needn't show every extreme that they name: `tile_lists`: entry 0 of each row is the tile's own index within its block of 4 tiles; the others are indices of the same or earlier tiles of that block. `expert_ids`: each row names 2 different experts; in the rows of one device no expert is named more than 128 times, and some expert reaches 128.
All inputs are finite; a program needn't handle non-finite values.
Results may differ from the reference program's by a relative error of at most 0.0047.
Values may be sent and summed in bfloat16 or wider, within the bound.
A program may use at most 64 MiB of HBM per device.

```python
import math
import jax
import jax.numpy as jnp
import numpy as np
from jax import lax

D = 1024
HEAD = 64
FF = 4096
TOPK = 2
TOK_DEV = 128
TILE = 32
LIST = 3
G_DEV = 4
EXPERTS = 4
CAP = 128
TOKENS = 1024
N_DEV = 8


def draw_queries(key, part):
    key = jax.random.fold_in(key, 7)
    drawn = jnp.clip(jax.random.normal(key, (TOKENS, D), jnp.float32), -6.0, 6.0)
    return drawn.astype(jnp.bfloat16)


def draw_keys(key, part):
    key = jax.random.fold_in(key, 9)
    drawn = jnp.clip(jax.random.normal(key, (TOKENS, D), jnp.float32), -6.0, 6.0)
    return drawn.astype(jnp.bfloat16)


def draw_tile_lists(key, part):
    key = jax.random.fold_in(key, 3)
    tile_count = TOK_DEV // TILE
    own_tile = (jnp.arange(TOKENS // TILE, dtype=jnp.int32) % tile_count).astype(jnp.int32)
    earlier = jax.random.randint(key, (TOKENS // TILE, LIST - 1), 0, 1 << 20, jnp.int32) % (own_tile[:, None] + 1)
    return jnp.concatenate([own_tile[:, None], earlier], axis=1).astype(jnp.int32)


def plant(values, rng, least, high):
    shape = values.shape
    spot = [jax.random.randint(jax.random.fold_in(rng, axis), (), 0, shape[axis]) for axis in range(len(shape))]
    values = values.at[tuple(spot)].set(least)
    longest = shape.index(max(shape))
    spot[longest] = (spot[longest] + 1) % shape[longest]
    return values.at[tuple(spot)].set(high)


def level_of(stream_key, extent, shards, low, high):
    gain, own = 1.0, jax.random.fold_in(stream_key, 6)
    for dim, parts in shards:
        heights = jnp.exp(jax.random.uniform(jax.random.fold_in(own, dim), (parts,), jnp.float32, low / len(shards), high / len(shards)))
        gain = gain * jnp.repeat(heights, extent[dim] // parts).reshape([-1 if axis == dim else 1 for axis in range(len(extent))])
    return gain


def split_up(number_of, total, reach, slope):
    portions = [(1 << 20) // math.isqrt(rank ** slope) + 1 for rank in range(2, number_of + 1)]
    spare, holding = total - reach - (number_of - 1), [1] * (number_of - 1)
    while spare > 0:
        movable = [i for i in range(number_of - 1) if holding[i] < reach]
        mass, remaining = sum([portions[i] for i in movable]), spare
        for i in movable:
            addition = min(reach - holding[i], max(1, remaining * portions[i] // mass), spare)
            holding[i] = holding[i] + addition
            spare = spare - addition
    return np.array([reach] + holding)


def ragged(rng, amount, total, limit, slope):
    if amount == 2:
        one = jax.random.randint(rng, (), max(1, total - limit), min(limit, total - 1) + 1)
        return jnp.stack([one, total - one])
    tallies = jnp.asarray(split_up(amount, total, limit, slope), jnp.int32)
    twos = (amount - 1) // 2
    donor, sink = tallies[1:1 + 2 * twos:2], tallies[2:2 + 2 * twos:2]
    room = jnp.minimum(donor - 1, limit - sink)
    passed = jax.random.randint(jax.random.fold_in(rng, 1), (twos,), 0, 1 << 20) % (room + 1)
    tallies = tallies.at[1:1 + 2 * twos:2].set(donor - passed).at[2:2 + 2 * twos:2].set(sink + passed)
    return tallies[jax.random.permutation(jax.random.fold_in(rng, 2), amount)]


def routed_block(rng, own, number, rows, amount, top, bound, slope):
    order = jax.random.permutation(rng, amount)
    heavy_load, ordinary = portions_of(amount, rows * top, bound, slope, True), portions_of(amount, rows * top, bound, slope, False)
    places = jnp.arange(amount)

    def named(sizes, rotation):
        used = int((sizes > 0).sum())
        fixed = max(1, used // 4)
        moved = fixed + (places - fixed + rotation * (used - fixed)) % max(1, amount - fixed)
        return jnp.zeros((amount,), jnp.int32).at[order[jnp.where(places < fixed, places, moved)]].set(jnp.asarray(sizes, jnp.int32))

    sizes = jnp.where(number % 4 == 0, named(heavy_load, number // 4), named(ordinary, number - number // 4 - 1))
    mixed = jax.random.permutation(jax.random.fold_in(own, 3), amount)
    donor, sink = mixed[0:amount // 2 * 2:2], mixed[1:amount // 2 * 2:2]
    room = jnp.minimum(sizes[donor] - 1, bound - sizes[sink]) // 2
    room = jnp.where((donor == order[0]) | (sink == order[0]) | (sizes[sink] == 0), 0, jnp.maximum(room, 0))
    moved = jax.random.randint(jax.random.fold_in(own, 4), (amount // 2,), 0, 1 << 20) % (room + 1)
    sizes = sizes.at[donor].add(-moved).at[sink].add(moved)
    members = jnp.searchsorted(jnp.cumsum(sizes), jnp.arange(rows * top), side="right").astype(jnp.int32)
    table = members.reshape(top, rows).T
    table = table[jax.random.permutation(jax.random.fold_in(own, 1), rows)]
    rotation = jax.random.randint(jax.random.fold_in(own, 2), (rows, 1), 0, top)
    return jnp.take_along_axis(table, (jnp.arange(top)[None, :] + rotation) % top, axis=1)


def portions_of(count, total, reach, slope, full):
    portions = [(1 << 20) // math.isqrt(rank ** slope) + 1 for rank in range(1, count + 1)]
    largest = reach if full else min(reach, max(-(-total // count), total * portions[0] // sum(portions)))
    least = 1 if total - largest >= count - 1 else 0
    holding, spare = [largest] + [least] * (count - 1), total - largest - least * (count - 1)
    while spare > 0:
        movable = [i for i in range(1, count) if holding[i] < largest] or [i for i in range(1, count) if holding[i] < reach]
        whole, budget = sum([portions[i] for i in movable]), spare
        for i in movable:
            addition = min(reach - holding[i], max(1, budget * portions[i] // whole), spare)
            holding[i] = holding[i] + addition
            spare = spare - addition
    return np.array(holding)


def noise(rng, shape, spread, reach, cuts=(), kind=jnp.bfloat16):
    level = level_of(rng, shape, cuts, -0.22, 0.18) if cuts else 1.0
    values = jax.random.normal(rng, shape, jnp.float32) * spread * level
    return jnp.minimum(jnp.maximum(values, -reach), reach).astype(kind)


def setup_inputs(seed: int = 0, part: int = 0) -> dict:
    streams_of = jax.random.split(jax.random.key(seed), 12)
    part_keys = jax.random.split(jax.random.fold_in(streams_of[11], part), 12)
    residual = noise(part_keys[0], (TOKENS, D), 1.0, 6.0, ((0, 8), (1, 2)))
    queries = draw_queries(jax.random.fold_in(jax.random.fold_in(streams_of[11], part), 71), part)
    keys = draw_keys(jax.random.fold_in(jax.random.fold_in(streams_of[11], part), 71), part)
    values = noise(part_keys[3], (TOKENS, D), 1.0, 6.0, ((0, 8), (1, 2)))
    tile_lists = draw_tile_lists(jax.random.fold_in(jax.random.fold_in(streams_of[11], part), 71), part)
    node_counts = jax.vmap(lambda own: ragged(own, G_DEV, TOK_DEV, TOK_DEV // 2, 2))(jax.random.split(part_keys[5], N_DEV)).reshape((N_DEV, G_DEV)).astype(jnp.int32)
    norm_gain = jnp.clip(1.0 + 0.1 * jax.random.normal(streams_of[6], (D,), jnp.float32), 0.5, 1.5)
    expert_ids_keys = jax.random.split(jax.random.fold_in(part_keys[7], 1), TOKENS // TOK_DEV)
    expert_ids_turns = jax.random.permutation(jax.random.fold_in(part_keys[7], 3), TOKENS // TOK_DEV)
    expert_ids = jax.vmap(lambda own, number: routed_block(jax.random.fold_in(part_keys[7], 2), own, number, TOK_DEV, EXPERTS, TOPK, CAP, 2))(expert_ids_keys, expert_ids_turns).reshape((TOKENS, TOPK))
    gate_codes = plant(jax.random.randint(part_keys[8], (TOKENS, TOPK), 8192, 57345), jax.random.fold_in(part_keys[8], 1), 8192, 57344).astype(jnp.int32)
    up_weight = noise(streams_of[9], (2 * EXPERTS, D, FF // 2), D ** -0.5, 0.1875, ((0, 8), (2, 2)))
    down_weight = noise(streams_of[10], (2 * EXPERTS, FF // 2, D), FF ** -0.5, 0.09375, ((0, 8), (1, 2)))
    return dict(residual=residual, queries=queries, keys=keys, values=values, tile_lists=tile_lists, node_counts=node_counts, norm_gain=norm_gain, expert_ids=expert_ids, gate_codes=gate_codes, up_weight=up_weight, down_weight=down_weight)


epsilon = 1e-06

def cone_mask(tile_lists, node_counts, node_total):
    tile_count = tile_lists.shape[0]
    tile_size = node_total // tile_count
    tile_ids = jnp.arange(tile_count, dtype=jnp.int32)
    tile_ok = jnp.any(tile_lists[:, :, None] == tile_ids[None, None, :], axis=1)
    node_ok = jnp.broadcast_to(tile_ok[:, None, :, None], (tile_count, tile_size, tile_count, tile_size)).reshape(node_total, node_total)
    nodes = jnp.arange(node_total, dtype=jnp.int32)
    graph_ends = jnp.cumsum(node_counts)
    graph_of = lax.optimization_barrier(jnp.sum((nodes[:, None] >= graph_ends[None, :]).astype(jnp.int32), axis=1))
    same_graph = graph_of[:, None] == graph_of[None, :]
    return node_ok & same_graph & (nodes[None, :] <= nodes[:, None])

def cone_attention(queries, keys, values, allowed):
    node_total, width = queries.shape
    head_count = width // HEAD
    query_heads = queries.reshape(node_total, head_count, HEAD).astype(jnp.float32)
    key_heads = keys.reshape(node_total, head_count, HEAD).astype(jnp.float32)
    value_heads = values.reshape(node_total, head_count, HEAD).astype(jnp.float32)
    scores = jnp.einsum('qhd,khd->hqk', query_heads, key_heads) * HEAD ** (-0.5)
    scores = jnp.where(allowed[None], scores, -1e+30)
    highest = lax.optimization_barrier(jnp.max(scores, axis=2, keepdims=True))
    weights = jnp.where(allowed[None], jnp.exp(scores - highest), 0.0)
    denominator = lax.optimization_barrier(jnp.sum(weights, axis=2, keepdims=True))
    probs = (weights / denominator).astype(jnp.bfloat16)
    attended = jnp.einsum('hqk,khd->qhd', probs.astype(jnp.float32), value_heads)
    return attended.reshape(node_total, width)

def slots_of(flat_ids, expert_count):
    onehot = (flat_ids[..., None] == jnp.arange(expert_count, dtype=jnp.int32)).astype(jnp.int32)
    before = jnp.cumsum(onehot, axis=-2) - onehot
    return lax.optimization_barrier(jnp.sum(before * onehot, axis=-1)).astype(jnp.int32)

def reference(residual, queries, keys, values, tile_lists, node_counts, norm_gain, expert_ids, gate_codes, up_weight, down_weight):
    tiles_dev = TOK_DEV // TILE

    def one_device(block):
        x_block, q_block, k_block, v_block, list_block, count_block = block
        allowed = cone_mask(list_block, count_block, TOK_DEV)
        return x_block.astype(jnp.float32) + cone_attention(q_block, k_block, v_block, allowed)
    stream = lax.map(one_device, (residual.reshape(N_DEV, TOK_DEV, D), queries.reshape(N_DEV, TOK_DEV, D), keys.reshape(N_DEV, TOK_DEV, D), values.reshape(N_DEV, TOK_DEV, D), tile_lists.reshape(N_DEV, tiles_dev, LIST), node_counts)).reshape(TOKENS, D)
    mean_square = lax.optimization_barrier(jnp.mean(stream * stream, axis=1, keepdims=True))
    normed = (stream * lax.rsqrt(mean_square + epsilon) * norm_gain).astype(jnp.bfloat16)
    flat_ids = expert_ids.reshape(N_DEV, TOK_DEV * TOPK)
    slot_index = slots_of(flat_ids, EXPERTS)
    sources = jnp.broadcast_to(jnp.arange(N_DEV, dtype=jnp.int32)[:, None], (N_DEV, TOK_DEV * TOPK))
    positions = (sources * CAP + slot_index).reshape(-1).astype(jnp.int32)
    owners = flat_ids.reshape(-1).astype(jnp.int32)
    node_of = (jnp.arange(TOKENS * TOPK, dtype=jnp.int32) // TOPK).astype(jnp.int32)
    table = jnp.full((EXPERTS, N_DEV * CAP), -1, jnp.int32).at[owners, positions].set(node_of)
    up_full = up_weight.reshape(EXPERTS, 2, D, FF // 2).transpose(0, 2, 1, 3).reshape(EXPERTS, D, FF)
    down_full = down_weight.reshape(EXPERTS, FF, D)

    def one_expert(block):
        rows_of, up_expert, down_expert = block
        picked = normed[jnp.maximum(rows_of, 0)] * (rows_of >= 0)[:, None].astype(jnp.bfloat16)
        pre_act = jnp.dot(picked, up_expert, preferred_element_type=jnp.float32)
        hidden = jax.nn.gelu(pre_act).astype(jnp.bfloat16)
        return jnp.dot(hidden, down_expert, preferred_element_type=jnp.float32).astype(jnp.bfloat16)
    outputs = lax.map(one_expert, (table, up_full, down_full))
    gathered = outputs[owners, positions].reshape(TOKENS, TOPK, D).astype(jnp.float32)
    gates = gate_codes.astype(jnp.float32) / 65536.0
    mixed = stream + lax.optimization_barrier(jnp.sum(gates[:, :, None] * gathered, axis=1))
    return mixed.astype(jnp.bfloat16)
```

```python
import functools

import jax
import jax.numpy as jnp
from jax import lax
from jax.experimental import pallas as pl
from jax.experimental.pallas import tpu as pltpu
from jax.sharding import PartitionSpec as P

D = 1024
HEAD = 64
TOPK = 2


epsilon = 1e-06


def from_partner(value, axis, bit):
    return lax.ppermute(value, axis, [(i, i ^ 1 << bit) for i in range(lax.axis_size(axis))])


def cone_mask(tile_lists, node_counts, node_total):
    tile_count = tile_lists.shape[0]
    tile_size = node_total // tile_count
    tile_ids = jnp.arange(tile_count, dtype=jnp.int32)
    tile_ok = jnp.any(tile_lists[:, :, None] == tile_ids[None, None, :], axis=1)
    node_ok = jnp.broadcast_to(
        tile_ok[:, None, :, None], (tile_count, tile_size, tile_count, tile_size)
    ).reshape(node_total, node_total)
    nodes = jnp.arange(node_total, dtype=jnp.int32)
    graph_ends = jnp.cumsum(node_counts)
    graph_of = jnp.sum((nodes[:, None] >= graph_ends[None, :]).astype(jnp.int32), axis=1)
    same_graph = graph_of[:, None] == graph_of[None, :]
    return node_ok & same_graph & (nodes[None, :] <= nodes[:, None])


def cone_attention(queries, keys, values, allowed):
    node_total, width = queries.shape
    head_count = width // HEAD
    query_heads = queries.reshape(node_total, head_count, HEAD)
    key_heads = keys.reshape(node_total, head_count, HEAD)
    value_heads = values.reshape(node_total, head_count, HEAD)
    scores = jnp.einsum(
        "qhd,khd->hqk", query_heads, key_heads, preferred_element_type=jnp.float32
    ) * HEAD ** (-0.5)
    scores = jnp.where(allowed[None], scores, -1e30)
    highest = jnp.max(scores, axis=2, keepdims=True)
    weights = jnp.where(allowed[None], jnp.exp(scores - highest), 0.0)
    denominator = jnp.sum(weights, axis=2, keepdims=True)
    probs = (weights / denominator).astype(jnp.bfloat16)
    attended = jnp.einsum("hqk,khd->qhd", probs, value_heads, preferred_element_type=jnp.float32)
    return attended.reshape(node_total, width)


def slots_of(flat_ids, expert_count):
    onehot = (flat_ids[..., None] == jnp.arange(expert_count, dtype=jnp.int32)).astype(jnp.int32)
    before = jnp.cumsum(onehot, axis=-2) - onehot
    return jnp.sum(before * onehot, axis=-1)


def per_device(
    residual,
    queries,
    keys,
    values,
    tile_lists,
    node_counts,
    norm_gain,
    expert_ids,
    gate_codes,
    up_weight,
    down_weight,
):
    node_total = residual.shape[0]
    half_width = residual.shape[1]
    quarter = half_width // 2
    devices = lax.axis_size("dev")
    experts = devices // 2
    capacity = 8 * node_total // devices
    parity = lax.axis_index("dev") % 2
    allowed = cone_mask(tile_lists, node_counts[0], node_total)
    stream = residual.astype(jnp.float32) + cone_attention(queries, keys, values, allowed)
    squares = lax.psum(jnp.sum(stream * stream, axis=1), "tp")
    normed = (stream * lax.rsqrt(squares / D + epsilon)[:, None] * norm_gain).astype(jnp.bfloat16)
    flat_ids = expert_ids.reshape(-1)
    slot_index = slots_of(flat_ids, experts)
    row_ids = jnp.arange(experts * capacity, dtype=jnp.int32)
    hits = (flat_ids[None, :] == (row_ids // capacity)[:, None]) & (
        slot_index[None, :] == (row_ids % capacity)[:, None]
    )
    dispatch = jnp.sum(
        hits.reshape(experts * capacity, node_total, TOPK).astype(jnp.int32), axis=2
    ).astype(jnp.bfloat16)
    packed = jnp.dot(dispatch, normed, preferred_element_type=jnp.float32).astype(jnp.bfloat16)
    outgoing = jnp.broadcast_to(
        packed.reshape(experts, 1, capacity, half_width), (experts, 2, capacity, half_width)
    ).reshape(devices * capacity, half_width)
    arrived = lax.all_to_all(outgoing, "dev", split_axis=0, concat_axis=0, tiled=True)
    w_up = up_weight[0]
    w_down = down_weight[0]
    up_whole, down_whole = (
        lax.all_gather(w_up, "tp", axis=1, tiled=True),
        lax.all_gather(w_down, "tp", axis=0, tiled=True),
    )
    served = lax.all_to_all(arrived, "tp", split_axis=0, concat_axis=1, tiled=True)
    hidden = jax.nn.gelu(jnp.dot(served, up_whole, preferred_element_type=jnp.float32)).astype(
        jnp.bfloat16
    )
    served_out = jnp.dot(hidden, down_whole, preferred_element_type=jnp.float32)
    summed_half = lax.all_to_all(served_out, "tp", split_axis=1, concat_axis=0, tiled=True)
    outgoing_share = lax.dynamic_slice_in_dim(summed_half, (1 - parity) * quarter, quarter, 1)
    kept_share = lax.dynamic_slice_in_dim(summed_half, parity * quarter, quarter, 1)
    finished = (
        kept_share
        + from_partner(outgoing_share.astype(jnp.bfloat16), "dev", 0).astype(outgoing_share.dtype)
    ).astype(jnp.bfloat16)
    returned = lax.all_to_all(finished, "dev", split_axis=0, concat_axis=1, tiled=True)
    returned = returned.reshape(capacity * experts, half_width)
    node_slots = slot_index.reshape(node_total, TOPK)
    gates = gate_codes.astype(jnp.float32) / 65536.0
    back_rows = jnp.arange(capacity * experts, dtype=jnp.int32)
    added = jnp.zeros((node_total, half_width), jnp.float32)
    for which in range(TOPK):
        picker = (
            (expert_ids[:, which][None, :] == (back_rows % experts)[:, None])
            & (node_slots[:, which][None, :] == (back_rows // experts)[:, None])
        ).astype(jnp.bfloat16)
        fetched = lax.dot_general(
            picker, returned, (((0,), (0,)), ((), ())), preferred_element_type=jnp.float32
        )
        added = added + gates[:, which : which + 1] * fetched
    return (stream + added).astype(jnp.bfloat16)


AUX = 128
LANES = 128


def pair_attention(query_pair, key_pair, value_pair, allowed, low_lanes):
    nodes = query_pair.shape[0]
    zero = jnp.zeros_like(query_pair)
    stacked = jnp.concatenate(
        [jnp.where(low_lanes, query_pair, zero), jnp.where(low_lanes, zero, query_pair)], axis=0
    )
    scores = lax.dot_general(
        stacked, key_pair, (((1,), (1,)), ((), ())), preferred_element_type=jnp.float32
    ) * HEAD ** (-0.5)
    scores = jnp.where(allowed, scores, -1e30)
    highest = jnp.max(scores, axis=1, keepdims=True)
    weights = jnp.where(allowed, jnp.exp(scores - highest), 0.0)
    denominator = jnp.sum(weights, axis=1, keepdims=True)
    probs = (weights / denominator).astype(jnp.bfloat16)
    both = jnp.dot(probs, value_pair, preferred_element_type=jnp.float32)
    return jnp.where(low_lanes, both[:nodes], both[nodes:])


def layer_kernel(
    rows_z,
    tile_ref,
    count_ref,
    residual_ref,
    query_ref,
    key_ref,
    value_ref,
    gain_ref,
    ids_ref,
    codes_ref,
    up_ref,
    down_ref,
    out_ref,
    gathered,
    stream,
    w_up,
    w_down,
    hidden,
    kept,
    a_out,
    a_in,
    b_out,
    b_in,
    c_out,
    c_in,
    w_sem,
    send_sem,
    piece_sem,
    a_sem,
    b_sem,
    c_sem,
):
    nodes, half = residual_ref.shape
    ff = up_ref.shape[2]
    width = 2 * half
    dev = lax.axis_index("dev")
    core = lax.axis_index("tp")
    z, x = dev // 2, dev % 2
    other_core = 1 - core
    other_x = 1 - x

    def z_of(step):
        flip = 0
        bit = 1
        while bit < rows_z:
            if step & bit:
                flip = flip + bit * (1 - 2 * ((z // bit) % 2))
            bit *= 2
        return z + flip

    load_up = pltpu.make_async_copy(up_ref.at[0], w_up, w_sem.at[0])
    load_down = pltpu.make_async_copy(down_ref.at[0], w_down, w_sem.at[1])
    load_up.start()
    load_down.start()

    barrier = pltpu.get_barrier_semaphore()
    to_core = {"tp": other_core}
    to_x = {"dev": 2 * z + other_x}
    to_z = [{"dev": 2 * z_of(step) + x} for step in range(rows_z)]
    peers = [to_core, to_x] + to_z[1:]
    for peer in peers:
        pl.semaphore_signal(barrier, inc=1, device_id=peer, device_id_type=pl.DeviceIdType.MESH)

    row = lax.broadcasted_iota(jnp.int32, (nodes, nodes), 0)
    column = lax.broadcasted_iota(jnp.int32, (nodes, nodes), 1)
    tile_count, listed = tile_ref.shape
    tile = nodes // tile_count
    column_tile = column // tile
    in_list = jnp.zeros((nodes, nodes), jnp.int32)
    for t in range(tile_count):
        hit = jnp.zeros((nodes, nodes), jnp.int32)
        for entry in range(listed):
            hit = jnp.where(column_tile == tile_ref[t, entry], 1, hit)
        in_list = jnp.where(row // tile == t, hit, in_list)
    row_graph = jnp.zeros((nodes, nodes), jnp.int32)
    column_graph = jnp.zeros((nodes, nodes), jnp.int32)
    end = 0
    for g in range(count_ref.shape[1]):
        end = end + count_ref[0, g]
        row_graph = row_graph + jnp.where(row >= end, 1, 0)
        column_graph = column_graph + jnp.where(column >= end, 1, 0)
    allowed_int = jnp.where((column <= row) & (row_graph == column_graph), in_list, 0)
    allowed = jnp.concatenate([allowed_int, allowed_int], axis=0) > 0
    low_lanes = lax.broadcasted_iota(jnp.int32, (nodes, LANES), 1) < HEAD

    own_rows = pl.ds(pl.multiple_of(x * nodes, nodes), nodes)
    other_rows = pl.ds(pl.multiple_of(other_x * nodes, nodes), nodes)

    squares = jnp.zeros((nodes, LANES), jnp.float32)
    for pair in range(half // LANES):
        lanes = slice(pair * LANES, (pair + 1) * LANES)
        attended = pair_attention(
            query_ref[:, lanes], key_ref[:, lanes], value_ref[:, lanes], allowed, low_lanes
        )
        part = residual_ref[:, lanes].astype(jnp.float32) + attended
        stream[:, lanes] = part
        squares = squares + part * part
        gathered[z, core, own_rows, lanes] = (part * gain_ref[:, lanes]).astype(jnp.bfloat16)

    lane = lax.broadcasted_iota(jnp.int32, (nodes, AUX), 1)
    total = jnp.sum(squares, axis=1, keepdims=True)
    item = lane // 2
    extra = jnp.where(item == rows_z, total, 0.0)
    for k in range(TOPK):
        gate = codes_ref[:, k : k + 1].astype(jnp.float32) / 65536.0
        extra = extra + jnp.where(item == ids_ref[:, k : k + 1], gate, 0.0)
    coarse = extra.astype(jnp.bfloat16)
    rest = (extra - coarse.astype(jnp.float32)).astype(jnp.bfloat16)
    gathered[z, core, own_rows, half:] = jnp.where(lane % 2 == 0, coarse.astype(jnp.float32), rest.astype(jnp.float32)).astype(jnp.bfloat16)

    def remote(src, dst, sent, received, device):
        return pltpu.make_async_remote_copy(
            src_ref=src,
            dst_ref=dst,
            send_sem=sent,
            recv_sem=received,
            device_id=device,
            device_id_type=pl.DeviceIdType.MESH,
        )

    def piece(zz, feature_half, xx, kind, step, device):
        rows = pl.ds(pl.multiple_of(xx * nodes, nodes), nodes)
        ref = gathered.at[zz, feature_half, rows]
        return remote(
            ref, ref, send_sem.at[kind, step], piece_sem.at[zz, feature_half, xx], device
        )

    started = []

    def start(copy):
        copy.start()
        started.append(copy)

    def spread(step):
        zz = z_of(step)
        if step:
            piece(zz, core, x, 0, step, to_z[step]).wait_recv()
        start(piece(zz, core, x, 1, step, to_x))
        start(piece(zz, core, x, 2, step, to_core))

    def spread_other(step):
        zz = z_of(step)
        piece(zz, core, other_x, 1, step, to_x).wait_recv()
        start(piece(zz, core, other_x, 3, step, to_core))

    def copy_a(step):
        return remote(
            a_out.at[step], a_in.at[step], send_sem.at[4, step], a_sem.at[step], to_core
        )

    def copy_b(step):
        return remote(b_out.at[step], b_in.at[step], send_sem.at[5, step], b_sem.at[step], to_x)

    def copy_c(step):
        return remote(
            c_out.at[step], c_in.at[step], send_sem.at[6, step], c_sem.at[step], to_z[step]
        )

    own_lanes = pl.ds(pl.multiple_of(core * half, half), half)
    other_lanes = pl.ds(pl.multiple_of(other_core * half, half), half)

    def compute(step):
        zz = z_of(step)
        piece(zz, other_core, x, 2, step, to_core).wait_recv()
        piece(zz, other_core, other_x, 3, step, to_core).wait_recv()
        aux_low = gathered[zz, 0, :, half:].astype(jnp.float32)
        aux_high = gathered[zz, 1, :, half:].astype(jnp.float32)
        item = lax.broadcasted_iota(jnp.int32, (2 * nodes, AUX), 1) // 2
        square = jnp.sum(jnp.where(item == rows_z, aux_low + aux_high, 0.0), axis=1, keepdims=True)
        scale = lax.rsqrt(square / width + epsilon)
        gate = jnp.sum(jnp.where(item == z, aux_low, 0.0), axis=1, keepdims=True)
        chunk = half

        @pl.loop(0, ff // chunk)
        def _(j):
            lanes = pl.ds(pl.multiple_of(j * chunk, chunk), chunk)
            pre = jnp.dot(
                gathered[zz, 0, :, :half], w_up[:half, lanes], preferred_element_type=jnp.float32
            ) + jnp.dot(
                gathered[zz, 1, :, :half], w_up[half:, lanes], preferred_element_type=jnp.float32
            )
            hidden[:, lanes] = jax.nn.gelu(pre * scale).astype(jnp.bfloat16)

        sent = jnp.dot(hidden[...], w_down[:, other_lanes], preferred_element_type=jnp.float32)
        a_out[step] = (sent * gate).astype(jnp.bfloat16)
        start(copy_a(step))
        stays = jnp.dot(hidden[...], w_down[:, own_lanes], preferred_element_type=jnp.float32)
        kept[step] = stays * gate

    def add_cores(step):
        copy_a(step).wait_recv()
        b_out[step] = (
            kept[step, other_rows] + a_in[step, other_rows].astype(jnp.float32)
        ).astype(jnp.bfloat16)
        start(copy_b(step))

    def add_columns(step):
        copy_b(step).wait_recv()
        total = (
            kept[step, own_rows]
            + a_in[step, own_rows].astype(jnp.float32)
            + b_in[step].astype(jnp.float32)
        )
        if step:
            c_out[step] = total.astype(jnp.bfloat16)
            start(copy_c(step))
        else:
            stream[...] += total

    pl.semaphore_wait(barrier, len(peers))
    for step in range(1, rows_z):
        start(piece(z, core, x, 0, step, to_z[step]))
    spread(0)
    spread_other(0)
    load_up.wait()
    load_down.wait()
    for step in range(rows_z + 2):
        if step + 1 < rows_z:
            spread(step + 1)
        if 1 <= step <= rows_z:
            add_cores(step - 1)
        if step < rows_z:
            compute(step)
        if step >= 2:
            add_columns(step - 2)
        if step + 1 < rows_z:
            spread_other(step + 1)

    result = stream[...]
    for step in range(1, rows_z):
        copy_c(step).wait_recv()
        result = result + c_in[step].astype(jnp.float32)
    out_ref[...] = result.astype(jnp.bfloat16)
    for copy in started:
        copy.wait_send()


def fused_device(
    residual,
    queries,
    keys,
    values,
    tile_lists,
    node_counts,
    norm_gain,
    expert_ids,
    gate_codes,
    up_weight,
    down_weight,
):
    nodes, half = residual.shape
    ff = up_weight.shape[2]
    rows_z = lax.axis_size("dev") // 2
    bf16, f32 = jnp.bfloat16, jnp.float32
    vmem = pl.BlockSpec(memory_space=pltpu.VMEM)
    smem = pl.BlockSpec(memory_space=pltpu.SMEM)
    hbm = pl.BlockSpec(memory_space=pl.ANY)
    return pl.pallas_call(
        functools.partial(layer_kernel, rows_z),
        out_shape=jax.ShapeDtypeStruct((nodes, half), bf16),
        in_specs=[smem, smem] + [vmem] * 7 + [hbm] * 2,
        out_specs=vmem,
        scratch_shapes=[
            pltpu.VMEM((rows_z, 2, 2 * nodes, half + AUX), bf16),
            pltpu.VMEM((nodes, half), f32),
            pltpu.VMEM(up_weight.shape[1:], bf16),
            pltpu.VMEM(down_weight.shape[1:], bf16),
            pltpu.VMEM((2 * nodes, ff), bf16),
            pltpu.VMEM((rows_z, 2 * nodes, half), f32),
            pltpu.VMEM((rows_z, 2 * nodes, half), bf16),
            pltpu.VMEM((rows_z, 2 * nodes, half), bf16),
            pltpu.VMEM((rows_z, nodes, half), bf16),
            pltpu.VMEM((rows_z, nodes, half), bf16),
            pltpu.VMEM((rows_z, nodes, half), bf16),
            pltpu.VMEM((rows_z, nodes, half), bf16),
            pltpu.SemaphoreType.DMA((2,)),
            pltpu.SemaphoreType.DMA((7, rows_z)),
            pltpu.SemaphoreType.DMA((rows_z, 2, 2)),
            pltpu.SemaphoreType.DMA((rows_z,)),
            pltpu.SemaphoreType.DMA((rows_z,)),
            pltpu.SemaphoreType.DMA((rows_z,)),
        ],
        compiler_params=pltpu.CompilerParams(
            collective_id=0, has_side_effects=True, vmem_limit_bytes=40 * 1024 * 1024
        ),
    )(
        tile_lists,
        node_counts,
        residual,
        queries,
        keys,
        values,
        norm_gain.reshape(1, half),
        expert_ids,
        gate_codes,
        up_weight,
        down_weight,
    )


def gathers_all(devices, nodes):
    experts = devices // 2
    capacity = 8 * nodes // devices
    return capacity >= nodes and experts & (experts - 1) == 0 and experts <= 8


def layer(residual, *others):
    if gathers_all(lax.axis_size("dev"), residual.shape[0]):
        return fused_device(residual, *others)
    return per_device(residual, *others)


def solution(mesh):
    in_specs = (
        P(("groups", "dev"), "tp"),
        P(("groups", "dev"), "tp"),
        P(("groups", "dev"), "tp"),
        P(("groups", "dev"), "tp"),
        P(("groups", "dev"), None),
        P(("groups", "dev"), None),
        P("tp"),
        P(("groups", "dev"), None),
        P(("groups", "dev"), None),
        P("dev", None, "tp"),
        P("dev", "tp", None),
    )
    out_specs = P(("groups", "dev"), "tp")
    return jax.shard_map(
        layer, mesh=mesh, in_specs=in_specs, out_specs=out_specs, check_vma=False
    )
```

```python
import functools

import jax
import jax.numpy as jnp
from jax import lax
from jax.experimental import pallas as pl
from jax.experimental.pallas import tpu as pltpu
from jax.sharding import PartitionSpec as P

D = 1024
HEAD = 64
TOPK = 2


epsilon = 1e-06


def from_partner(value, axis, bit):
    return lax.ppermute(value, axis, [(i, i ^ 1 << bit) for i in range(lax.axis_size(axis))])


def cone_mask(tile_lists, node_counts, node_total):
    tile_count = tile_lists.shape[0]
    tile_size = node_total // tile_count
    tile_ids = jnp.arange(tile_count, dtype=jnp.int32)
    tile_ok = jnp.any(tile_lists[:, :, None] == tile_ids[None, None, :], axis=1)
    node_ok = jnp.broadcast_to(
        tile_ok[:, None, :, None], (tile_count, tile_size, tile_count, tile_size)
    ).reshape(node_total, node_total)
    nodes = jnp.arange(node_total, dtype=jnp.int32)
    graph_ends = jnp.cumsum(node_counts)
    graph_of = jnp.sum((nodes[:, None] >= graph_ends[None, :]).astype(jnp.int32), axis=1)
    same_graph = graph_of[:, None] == graph_of[None, :]
    return node_ok & same_graph & (nodes[None, :] <= nodes[:, None])


def cone_attention(queries, keys, values, allowed):
    node_total, width = queries.shape
    head_count = width // HEAD
    query_heads = queries.reshape(node_total, head_count, HEAD)
    key_heads = keys.reshape(node_total, head_count, HEAD)
    value_heads = values.reshape(node_total, head_count, HEAD)
    scores = jnp.einsum(
        "qhd,khd->hqk", query_heads, key_heads, preferred_element_type=jnp.float32
    ) * HEAD ** (-0.5)
    scores = jnp.where(allowed[None], scores, -1e30)
    highest = jnp.max(scores, axis=2, keepdims=True)
    weights = jnp.where(allowed[None], jnp.exp(scores - highest), 0.0)
    denominator = jnp.sum(weights, axis=2, keepdims=True)
    probs = (weights / denominator).astype(jnp.bfloat16)
    attended = jnp.einsum("hqk,khd->qhd", probs, value_heads, preferred_element_type=jnp.float32)
    return attended.reshape(node_total, width)


def slots_of(flat_ids, expert_count):
    onehot = (flat_ids[..., None] == jnp.arange(expert_count, dtype=jnp.int32)).astype(jnp.int32)
    before = jnp.cumsum(onehot, axis=-2) - onehot
    return jnp.sum(before * onehot, axis=-1)


def per_device(
    residual,
    queries,
    keys,
    values,
    tile_lists,
    node_counts,
    norm_gain,
    expert_ids,
    gate_codes,
    up_weight,
    down_weight,
):
    node_total = residual.shape[0]
    half_width = residual.shape[1]
    quarter = half_width // 2
    devices = lax.axis_size("dev")
    experts = devices // 2
    capacity = 8 * node_total // devices
    parity = lax.axis_index("dev") % 2
    allowed = cone_mask(tile_lists, node_counts[0], node_total)
    stream = residual.astype(jnp.float32) + cone_attention(queries, keys, values, allowed)
    squares = lax.psum(jnp.sum(stream * stream, axis=1), "tp")
    normed = (stream * lax.rsqrt(squares / D + epsilon)[:, None] * norm_gain).astype(jnp.bfloat16)
    flat_ids = expert_ids.reshape(-1)
    slot_index = slots_of(flat_ids, experts)
    row_ids = jnp.arange(experts * capacity, dtype=jnp.int32)
    hits = (flat_ids[None, :] == (row_ids // capacity)[:, None]) & (
        slot_index[None, :] == (row_ids % capacity)[:, None]
    )
    dispatch = jnp.sum(
        hits.reshape(experts * capacity, node_total, TOPK).astype(jnp.int32), axis=2
    ).astype(jnp.bfloat16)
    packed = jnp.dot(dispatch, normed, preferred_element_type=jnp.float32).astype(jnp.bfloat16)
    outgoing = jnp.broadcast_to(
        packed.reshape(experts, 1, capacity, half_width), (experts, 2, capacity, half_width)
    ).reshape(devices * capacity, half_width)
    arrived = lax.all_to_all(outgoing, "dev", split_axis=0, concat_axis=0, tiled=True)
    w_up = up_weight[0]
    w_down = down_weight[0]
    up_whole, down_whole = (
        lax.all_gather(w_up, "tp", axis=1, tiled=True),
        lax.all_gather(w_down, "tp", axis=0, tiled=True),
    )
    served = lax.all_to_all(arrived, "tp", split_axis=0, concat_axis=1, tiled=True)
    hidden = jax.nn.gelu(jnp.dot(served, up_whole, preferred_element_type=jnp.float32)).astype(
        jnp.bfloat16
    )
    served_out = jnp.dot(hidden, down_whole, preferred_element_type=jnp.float32)
    summed_half = lax.all_to_all(served_out, "tp", split_axis=1, concat_axis=0, tiled=True)
    outgoing_share = lax.dynamic_slice_in_dim(summed_half, (1 - parity) * quarter, quarter, 1)
    kept_share = lax.dynamic_slice_in_dim(summed_half, parity * quarter, quarter, 1)
    finished = (
        kept_share
        + from_partner(outgoing_share.astype(jnp.bfloat16), "dev", 0).astype(outgoing_share.dtype)
    ).astype(jnp.bfloat16)
    returned = lax.all_to_all(finished, "dev", split_axis=0, concat_axis=1, tiled=True)
    returned = returned.reshape(capacity * experts, half_width)
    node_slots = slot_index.reshape(node_total, TOPK)
    gates = gate_codes.astype(jnp.float32) / 65536.0
    back_rows = jnp.arange(capacity * experts, dtype=jnp.int32)
    added = jnp.zeros((node_total, half_width), jnp.float32)
    for which in range(TOPK):
        picker = (
            (expert_ids[:, which][None, :] == (back_rows % experts)[:, None])
            & (node_slots[:, which][None, :] == (back_rows // experts)[:, None])
        ).astype(jnp.bfloat16)
        fetched = lax.dot_general(
            picker, returned, (((0,), (0,)), ((), ())), preferred_element_type=jnp.float32
        )
        added = added + gates[:, which : which + 1] * fetched
    return (stream + added).astype(jnp.bfloat16)


AUX = 16
LANES = 128


def pair_attention(query_pair, key_pair, value_pair, allowed, low_lanes):
    nodes = query_pair.shape[0]
    zero = jnp.zeros_like(query_pair)
    stacked = jnp.concatenate(
        [jnp.where(low_lanes, query_pair, zero), jnp.where(low_lanes, zero, query_pair)], axis=0
    )
    scores = lax.dot_general(
        stacked, key_pair, (((1,), (1,)), ((), ())), preferred_element_type=jnp.float32
    ) * HEAD ** (-0.5)
    scores = jnp.where(allowed, scores, -1e30)
    highest = jnp.max(scores, axis=1, keepdims=True)
    weights = jnp.where(allowed, jnp.exp(scores - highest), 0.0)
    denominator = jnp.sum(weights, axis=1, keepdims=True)
    probs = (weights / denominator).astype(jnp.bfloat16)
    both = jnp.dot(probs, value_pair, preferred_element_type=jnp.float32)
    return jnp.where(low_lanes, both[:nodes], both[nodes:])


def layer_kernel(
    rows_z,
    tile_hbm,
    count_hbm,
    residual_hbm,
    query_hbm,
    key_hbm,
    value_hbm,
    gain_hbm,
    ids_hbm,
    codes_hbm,
    up_ref,
    down_ref,
    out_ref,
    tile_ref,
    count_ref,
    residual_ref,
    query_ref,
    key_ref,
    value_ref,
    gain_ref,
    ids_ref,
    codes_ref,
    gathered,
    stream,
    w_up,
    w_down,
    hidden,
    kept,
    a_out,
    a_in,
    b_out,
    b_in,
    c_out,
    c_in,
    w_sem,
    send_sem,
    piece_sem,
    a_sem,
    b_sem,
    c_sem,
):
    nodes, half = residual_ref.shape
    ff = up_ref.shape[2]
    width = 2 * half
    dev = lax.axis_index("dev")
    core = lax.axis_index("tp")
    z, x = dev // 2, dev % 2
    other_core = 1 - core
    other_x = 1 - x

    def z_of(step):
        flip = 0
        bit = 1
        while bit < rows_z:
            if step & bit:
                flip = flip + bit * (1 - 2 * ((z // bit) % 2))
            bit *= 2
        return z + flip

    small = []
    for hbm, near in (
        (tile_hbm, tile_ref),
        (count_hbm, count_ref),
        (query_hbm, query_ref),
        (key_hbm, key_ref),
        (value_hbm, value_ref),
        (residual_hbm, residual_ref),
        (gain_hbm, gain_ref),
        (ids_hbm, ids_ref),
        (codes_hbm, codes_ref),
    ):
        copy = pltpu.make_async_copy(hbm, near, w_sem.at[2 + len(small)])
        copy.start()
        small.append(copy)
    load_up = pltpu.make_async_copy(up_ref.at[0], w_up, w_sem.at[0])
    load_down = pltpu.make_async_copy(down_ref.at[0], w_down, w_sem.at[1])
    load_up.start()
    load_down.start()

    barrier = pltpu.get_barrier_semaphore()
    to_core = {"tp": other_core}
    to_x = {"dev": 2 * z + other_x}
    to_z = [{"dev": 2 * z_of(step) + x} for step in range(rows_z)]
    peers = [to_core, to_x] + to_z[1:]
    for peer in peers:
        pl.semaphore_signal(barrier, inc=1, device_id=peer, device_id_type=pl.DeviceIdType.MESH)

    for copy in small:
        copy.wait()

    row = lax.broadcasted_iota(jnp.int32, (nodes, nodes), 0)
    column = lax.broadcasted_iota(jnp.int32, (nodes, nodes), 1)
    tile_count, listed = tile_ref.shape
    tile = nodes // tile_count
    column_tile = column // tile
    in_list = jnp.zeros((nodes, nodes), jnp.int32)
    for t in range(tile_count):
        hit = jnp.zeros((nodes, nodes), jnp.int32)
        for entry in range(listed):
            hit = jnp.where(column_tile == tile_ref[t, entry], 1, hit)
        in_list = jnp.where(row // tile == t, hit, in_list)
    row_graph = jnp.zeros((nodes, nodes), jnp.int32)
    column_graph = jnp.zeros((nodes, nodes), jnp.int32)
    end = 0
    for g in range(count_ref.shape[1]):
        end = end + count_ref[0, g]
        row_graph = row_graph + jnp.where(row >= end, 1, 0)
        column_graph = column_graph + jnp.where(column >= end, 1, 0)
    allowed_int = jnp.where((column <= row) & (row_graph == column_graph), in_list, 0)
    allowed = jnp.concatenate([allowed_int, allowed_int], axis=0) > 0
    low_lanes = lax.broadcasted_iota(jnp.int32, (nodes, LANES), 1) < HEAD

    own_rows = pl.ds(pl.multiple_of(x * nodes, nodes), nodes)
    other_rows = pl.ds(pl.multiple_of(other_x * nodes, nodes), nodes)

    squares = jnp.zeros((nodes, LANES), jnp.float32)
    for pair in range(half // LANES):
        lanes = slice(pair * LANES, (pair + 1) * LANES)
        attended = pair_attention(
            query_ref[:, lanes], key_ref[:, lanes], value_ref[:, lanes], allowed, low_lanes
        )
        part = residual_ref[:, lanes].astype(jnp.float32) + attended
        stream[:, lanes] = part
        squares = squares + part * part
        gathered[z, core, x, :nodes, lanes] = (part * gain_ref[:, lanes]).astype(jnp.bfloat16)

    item = lax.broadcasted_iota(jnp.int32, (AUX, nodes), 0)
    total = jnp.sum(squares.T, axis=0, keepdims=True)
    extra = jnp.where(item // 2 == rows_z, total, 0.0)
    for k in range(TOPK):
        gate = codes_ref[k : k + 1, :].astype(jnp.float32) / 65536.0
        extra = extra + jnp.where(item // 2 == ids_ref[k : k + 1, :], gate, 0.0)
    coarse = extra.astype(jnp.bfloat16).astype(jnp.float32)
    extra = jnp.where(item % 2 == 0, coarse, extra - coarse).astype(jnp.bfloat16)
    gathered[z, core, x, nodes:, :LANES] = extra
    for pair in range(1, half // LANES):
        lanes = slice(pair * LANES, (pair + 1) * LANES)
        gathered[z, core, x, nodes:, lanes] = jnp.zeros((AUX, LANES), jnp.bfloat16)

    def remote(src, dst, sent, received, device):
        return pltpu.make_async_remote_copy(
            src_ref=src,
            dst_ref=dst,
            send_sem=sent,
            recv_sem=received,
            device_id=device,
            device_id_type=pl.DeviceIdType.MESH,
        )

    def piece(zz, feature_half, xx, kind, step, device):
        ref = gathered.at[zz, feature_half, xx]
        return remote(
            ref, ref, send_sem.at[kind, step], piece_sem.at[zz, feature_half, xx], device
        )

    started = []

    def start(copy):
        copy.start()
        started.append(copy)

    def spread(step):
        zz = z_of(step)
        if step:
            piece(zz, core, x, 0, step, to_z[step]).wait_recv()
        start(piece(zz, core, x, 1, step, to_x))
        start(piece(zz, core, x, 2, step, to_core))

    def spread_other(step):
        zz = z_of(step)
        piece(zz, core, other_x, 1, step, to_x).wait_recv()
        start(piece(zz, core, other_x, 3, step, to_core))

    def copy_a(step):
        return remote(
            a_out.at[step], a_in.at[step], send_sem.at[4, step], a_sem.at[step], to_core
        )

    def copy_b(step):
        return remote(b_out.at[step], b_in.at[step], send_sem.at[5, step], b_sem.at[step], to_x)

    def copy_c(step):
        return remote(
            c_out.at[step], c_in.at[step], send_sem.at[6, step], c_sem.at[step], to_z[step]
        )

    own_lanes = pl.ds(pl.multiple_of(core * half, half), half)
    other_lanes = pl.ds(pl.multiple_of(other_core * half, half), half)

    def compute(step):
        zz = z_of(step)
        piece(zz, other_core, x, 2, step, to_core).wait_recv()
        piece(zz, other_core, other_x, 3, step, to_core).wait_recv()
        item = lax.broadcasted_iota(jnp.int32, (AUX, LANES), 0) // 2
        pick_square = jnp.where(item == rows_z, 1.0, 0.0).astype(jnp.bfloat16)
        pick_gate = jnp.where(item == z, 1.0, 0.0).astype(jnp.bfloat16)

        def column_of(feature_half, pick):
            return jnp.concatenate(
                [
                    lax.dot_general(
                        gathered[zz, feature_half, xx, nodes:, :LANES],
                        pick,
                        (((0,), (0,)), ((), ())),
                        preferred_element_type=jnp.float32,
                    )[:, :1]
                    for xx in range(2)
                ],
                axis=0,
            )

        def rows_of(feature_half):
            return jnp.concatenate(
                [gathered[zz, feature_half, xx, :nodes] for xx in range(2)], axis=0
            )

        square = column_of(0, pick_square) + column_of(1, pick_square)
        scale = lax.rsqrt(square / width + epsilon)
        gate = column_of(0, pick_gate)
        chunk = half

        @pl.loop(0, ff // chunk)
        def _(j):
            lanes = pl.ds(pl.multiple_of(j * chunk, chunk), chunk)
            pre = jnp.dot(
                rows_of(0), w_up[:half, lanes], preferred_element_type=jnp.float32
            ) + jnp.dot(
                rows_of(1), w_up[half:, lanes], preferred_element_type=jnp.float32
            )
            hidden[:, lanes] = jax.nn.gelu(pre * scale).astype(jnp.bfloat16)

        sent = jnp.dot(hidden[...], w_down[:, other_lanes], preferred_element_type=jnp.float32)
        a_out[step] = (sent * gate).astype(jnp.bfloat16)
        start(copy_a(step))
        stays = jnp.dot(hidden[...], w_down[:, own_lanes], preferred_element_type=jnp.float32)
        kept[step] = stays * gate

    def add_cores(step):
        copy_a(step).wait_recv()
        b_out[step] = (
            kept[step, other_rows] + a_in[step, other_rows].astype(jnp.float32)
        ).astype(jnp.bfloat16)
        start(copy_b(step))

    def add_columns(step):
        copy_b(step).wait_recv()
        total = (
            kept[step, own_rows]
            + a_in[step, own_rows].astype(jnp.float32)
            + b_in[step].astype(jnp.float32)
        )
        if step:
            c_out[step] = total.astype(jnp.bfloat16)
            start(copy_c(step))
        else:
            stream[...] += total

    pl.semaphore_wait(barrier, len(peers))
    for step in range(1, rows_z):
        start(piece(z, core, x, 0, step, to_z[step]))
    spread(0)
    spread_other(0)
    load_up.wait()
    load_down.wait()
    for step in range(rows_z + 2):
        if step + 1 < rows_z:
            spread(step + 1)
        if 1 <= step <= rows_z:
            add_cores(step - 1)
        if step < rows_z:
            compute(step)
        if step >= 2:
            add_columns(step - 2)
        if step + 1 < rows_z:
            spread_other(step + 1)

    result = stream[...]
    for step in range(1, rows_z):
        copy_c(step).wait_recv()
        result = result + c_in[step].astype(jnp.float32)
    out_ref[...] = result.astype(jnp.bfloat16)
    for copy in started:
        copy.wait_send()


def fused_device(
    residual,
    queries,
    keys,
    values,
    tile_lists,
    node_counts,
    norm_gain,
    expert_ids,
    gate_codes,
    up_weight,
    down_weight,
):
    nodes, half = residual.shape
    ff = up_weight.shape[2]
    rows_z = lax.axis_size("dev") // 2
    bf16, f32 = jnp.bfloat16, jnp.float32
    hbm = pl.BlockSpec(memory_space=pl.ANY)
    return pl.pallas_call(
        functools.partial(layer_kernel, rows_z),
        out_shape=jax.ShapeDtypeStruct((nodes, half), bf16),
        in_specs=[hbm] * 11,
        out_specs=pl.BlockSpec(memory_space=pltpu.VMEM),
        scratch_shapes=[
            pltpu.SMEM(tile_lists.shape, jnp.int32),
            pltpu.SMEM(node_counts.shape, jnp.int32),
            pltpu.VMEM((nodes, half), bf16),
            pltpu.VMEM((nodes, half), bf16),
            pltpu.VMEM((nodes, half), bf16),
            pltpu.VMEM((nodes, half), bf16),
            pltpu.VMEM((1, half), f32),
            pltpu.VMEM((TOPK, nodes), jnp.int32),
            pltpu.VMEM((TOPK, nodes), jnp.int32),
            pltpu.VMEM((rows_z, 2, 2, nodes + AUX, half), bf16),
            pltpu.VMEM((nodes, half), f32),
            pltpu.VMEM(up_weight.shape[1:], bf16),
            pltpu.VMEM(down_weight.shape[1:], bf16),
            pltpu.VMEM((2 * nodes, ff), bf16),
            pltpu.VMEM((rows_z, 2 * nodes, half), f32),
            pltpu.VMEM((rows_z, 2 * nodes, half), bf16),
            pltpu.VMEM((rows_z, 2 * nodes, half), bf16),
            pltpu.VMEM((rows_z, nodes, half), bf16),
            pltpu.VMEM((rows_z, nodes, half), bf16),
            pltpu.VMEM((rows_z, nodes, half), bf16),
            pltpu.VMEM((rows_z, nodes, half), bf16),
            pltpu.SemaphoreType.DMA((11,)),
            pltpu.SemaphoreType.DMA((7, rows_z)),
            pltpu.SemaphoreType.DMA((rows_z, 2, 2)),
            pltpu.SemaphoreType.DMA((rows_z,)),
            pltpu.SemaphoreType.DMA((rows_z,)),
            pltpu.SemaphoreType.DMA((rows_z,)),
        ],
        compiler_params=pltpu.CompilerParams(
            collective_id=0, has_side_effects=True, vmem_limit_bytes=63 * 1024 * 1024
        ),
    )(
        tile_lists,
        node_counts,
        residual,
        queries,
        keys,
        values,
        norm_gain.reshape(1, half),
        expert_ids.T,
        gate_codes.T,
        up_weight,
        down_weight,
    )


def gathers_all(devices, nodes):
    experts = devices // 2
    capacity = 8 * nodes // devices
    return capacity >= nodes and experts & (experts - 1) == 0 and experts < 8


def layer(residual, *others):
    if gathers_all(lax.axis_size("dev"), residual.shape[0]):
        return fused_device(residual, *others)
    return per_device(residual, *others)


def solution(mesh):
    in_specs = (
        P(("groups", "dev"), "tp"),
        P(("groups", "dev"), "tp"),
        P(("groups", "dev"), "tp"),
        P(("groups", "dev"), "tp"),
        P(("groups", "dev"), None),
        P(("groups", "dev"), None),
        P("tp"),
        P(("groups", "dev"), None),
        P(("groups", "dev"), None),
        P("dev", None, "tp"),
        P("dev", "tp", None),
    )
    out_specs = P(("groups", "dev"), "tp")
    return jax.shard_map(
        layer, mesh=mesh, in_specs=in_specs, out_specs=out_specs, check_vma=False
    )
```

```python
import functools

import jax
import jax.numpy as jnp
from jax import lax
from jax.experimental import pallas as pl
from jax.experimental.pallas import tpu as pltpu
from jax.sharding import PartitionSpec as P

D = 1024
HEAD = 64
TOPK = 2


epsilon = 1e-06


def from_partner(value, axis, bit):
    return lax.ppermute(value, axis, [(i, i ^ 1 << bit) for i in range(lax.axis_size(axis))])


def cone_mask(tile_lists, node_counts, node_total):
    tile_count = tile_lists.shape[0]
    tile_size = node_total // tile_count
    tile_ids = jnp.arange(tile_count, dtype=jnp.int32)
    tile_ok = jnp.any(tile_lists[:, :, None] == tile_ids[None, None, :], axis=1)
    node_ok = jnp.broadcast_to(
        tile_ok[:, None, :, None], (tile_count, tile_size, tile_count, tile_size)
    ).reshape(node_total, node_total)
    nodes = jnp.arange(node_total, dtype=jnp.int32)
    graph_ends = jnp.cumsum(node_counts)
    graph_of = jnp.sum((nodes[:, None] >= graph_ends[None, :]).astype(jnp.int32), axis=1)
    same_graph = graph_of[:, None] == graph_of[None, :]
    return node_ok & same_graph & (nodes[None, :] <= nodes[:, None])


def cone_attention(queries, keys, values, allowed):
    node_total, width = queries.shape
    head_count = width // HEAD
    query_heads = queries.reshape(node_total, head_count, HEAD)
    key_heads = keys.reshape(node_total, head_count, HEAD)
    value_heads = values.reshape(node_total, head_count, HEAD)
    scores = jnp.einsum(
        "qhd,khd->hqk", query_heads, key_heads, preferred_element_type=jnp.float32
    ) * HEAD ** (-0.5)
    scores = jnp.where(allowed[None], scores, -1e30)
    highest = jnp.max(scores, axis=2, keepdims=True)
    weights = jnp.where(allowed[None], jnp.exp(scores - highest), 0.0)
    denominator = jnp.sum(weights, axis=2, keepdims=True)
    probs = (weights / denominator).astype(jnp.bfloat16)
    attended = jnp.einsum("hqk,khd->qhd", probs, value_heads, preferred_element_type=jnp.float32)
    return attended.reshape(node_total, width)


def slots_of(flat_ids, expert_count):
    onehot = (flat_ids[..., None] == jnp.arange(expert_count, dtype=jnp.int32)).astype(jnp.int32)
    before = jnp.cumsum(onehot, axis=-2) - onehot
    return jnp.sum(before * onehot, axis=-1)


def per_device(
    residual,
    queries,
    keys,
    values,
    tile_lists,
    node_counts,
    norm_gain,
    expert_ids,
    gate_codes,
    up_weight,
    down_weight,
):
    node_total = residual.shape[0]
    half_width = residual.shape[1]
    quarter = half_width // 2
    devices = lax.axis_size("dev")
    experts = devices // 2
    capacity = 8 * node_total // devices
    parity = lax.axis_index("dev") % 2
    allowed = cone_mask(tile_lists, node_counts[0], node_total)
    stream = residual.astype(jnp.float32) + cone_attention(queries, keys, values, allowed)
    squares = lax.psum(jnp.sum(stream * stream, axis=1), "tp")
    normed = (stream * lax.rsqrt(squares / D + epsilon)[:, None] * norm_gain).astype(jnp.bfloat16)
    flat_ids = expert_ids.reshape(-1)
    slot_index = slots_of(flat_ids, experts)
    row_ids = jnp.arange(experts * capacity, dtype=jnp.int32)
    hits = (flat_ids[None, :] == (row_ids // capacity)[:, None]) & (
        slot_index[None, :] == (row_ids % capacity)[:, None]
    )
    dispatch = jnp.sum(
        hits.reshape(experts * capacity, node_total, TOPK).astype(jnp.int32), axis=2
    ).astype(jnp.bfloat16)
    packed = jnp.dot(dispatch, normed, preferred_element_type=jnp.float32).astype(jnp.bfloat16)
    outgoing = jnp.broadcast_to(
        packed.reshape(experts, 1, capacity, half_width), (experts, 2, capacity, half_width)
    ).reshape(devices * capacity, half_width)
    arrived = lax.all_to_all(outgoing, "dev", split_axis=0, concat_axis=0, tiled=True)
    w_up = up_weight[0]
    w_down = down_weight[0]
    up_whole, down_whole = (
        lax.all_gather(w_up, "tp", axis=1, tiled=True),
        lax.all_gather(w_down, "tp", axis=0, tiled=True),
    )
    served = lax.all_to_all(arrived, "tp", split_axis=0, concat_axis=1, tiled=True)
    hidden = jax.nn.gelu(jnp.dot(served, up_whole, preferred_element_type=jnp.float32)).astype(
        jnp.bfloat16
    )
    served_out = jnp.dot(hidden, down_whole, preferred_element_type=jnp.float32)
    summed_half = lax.all_to_all(served_out, "tp", split_axis=1, concat_axis=0, tiled=True)
    outgoing_share = lax.dynamic_slice_in_dim(summed_half, (1 - parity) * quarter, quarter, 1)
    kept_share = lax.dynamic_slice_in_dim(summed_half, parity * quarter, quarter, 1)
    finished = (
        kept_share
        + from_partner(outgoing_share.astype(jnp.bfloat16), "dev", 0).astype(outgoing_share.dtype)
    ).astype(jnp.bfloat16)
    returned = lax.all_to_all(finished, "dev", split_axis=0, concat_axis=1, tiled=True)
    returned = returned.reshape(capacity * experts, half_width)
    node_slots = slot_index.reshape(node_total, TOPK)
    gates = gate_codes.astype(jnp.float32) / 65536.0
    back_rows = jnp.arange(capacity * experts, dtype=jnp.int32)
    added = jnp.zeros((node_total, half_width), jnp.float32)
    for which in range(TOPK):
        picker = (
            (expert_ids[:, which][None, :] == (back_rows % experts)[:, None])
            & (node_slots[:, which][None, :] == (back_rows // experts)[:, None])
        ).astype(jnp.bfloat16)
        fetched = lax.dot_general(
            picker, returned, (((0,), (0,)), ((), ())), preferred_element_type=jnp.float32
        )
        added = added + gates[:, which : which + 1] * fetched
    return (stream + added).astype(jnp.bfloat16)


AUX = 16
CHUNKS = 2
LANES = 128


def pair_attention(query_pair, key_pair, value_pair, allowed, low_lanes):
    nodes = query_pair.shape[0]
    zero = jnp.zeros_like(query_pair)
    stacked = jnp.concatenate(
        [jnp.where(low_lanes, query_pair, zero), jnp.where(low_lanes, zero, query_pair)], axis=0
    )
    scores = lax.dot_general(
        stacked, key_pair, (((1,), (1,)), ((), ())), preferred_element_type=jnp.float32
    ) * HEAD ** (-0.5)
    scores = jnp.where(allowed, scores, -1e30)
    highest = jnp.max(scores, axis=1, keepdims=True)
    weights = jnp.where(allowed, jnp.exp(scores - highest), 0.0)
    denominator = jnp.sum(weights, axis=1, keepdims=True)
    probs = (weights / denominator).astype(jnp.bfloat16)
    both = jnp.dot(probs, value_pair, preferred_element_type=jnp.float32)
    return jnp.where(low_lanes, both[:nodes], both[nodes:])


def layer_kernel(
    rows_z,
    tile_hbm,
    count_hbm,
    residual_hbm,
    query_hbm,
    key_hbm,
    value_hbm,
    gain_hbm,
    ids_hbm,
    codes_hbm,
    up_ref,
    down_ref,
    out_ref,
    tile_ref,
    count_ref,
    residual_ref,
    query_ref,
    key_ref,
    value_ref,
    gain_ref,
    ids_ref,
    codes_ref,
    gathered,
    stream,
    w_up,
    w_down,
    hidden,
    kept,
    a_out,
    a_in,
    b_out,
    b_in,
    c_out,
    c_in,
    w_sem,
    send_sem,
    piece_sem,
    a_sem,
    b_sem,
    c_sem,
):
    nodes, half = residual_ref.shape
    ff = up_ref.shape[2]
    width = 2 * half
    dev = lax.axis_index("dev")
    core = lax.axis_index("tp")
    z, x = dev // 2, dev % 2
    other_core = 1 - core
    other_x = 1 - x

    orders = []
    for place in range(rows_z):
        order = [place]
        for distance in range(1, rows_z):
            order += [r for r in (place + distance, place - distance) if 0 <= r < rows_z]
        orders.append(order)

    def z_of(step):
        found = orders[0][step]
        for place in range(1, rows_z):
            found = jnp.where(z == place, orders[place][step], found)
        return found

    z_order = [z] + [z_of(step) for step in range(1, rows_z)]

    small = []
    for hbm, near in (
        (tile_hbm, tile_ref),
        (count_hbm, count_ref),
        (query_hbm, query_ref),
        (key_hbm, key_ref),
        (value_hbm, value_ref),
        (residual_hbm, residual_ref),
        (gain_hbm, gain_ref),
        (ids_hbm, ids_ref),
        (codes_hbm, codes_ref),
    ):
        copy = pltpu.make_async_copy(hbm, near, w_sem.at[2 + len(small)])
        copy.start()
        small.append(copy)
    load_up = pltpu.make_async_copy(up_ref.at[0], w_up, w_sem.at[0])
    load_down = pltpu.make_async_copy(down_ref.at[0], w_down, w_sem.at[1])
    load_up.start()
    load_down.start()

    barrier = pltpu.get_barrier_semaphore()
    to_core = {"tp": other_core}
    to_x = {"dev": 2 * z + other_x}
    to_z = [{"dev": 2 * zz + x} for zz in z_order]
    to_above, to_below = {"dev": dev + 2}, {"dev": dev - 2}
    peers = [to_core, to_x] + to_z[1:]
    for peer in peers:
        pl.semaphore_signal(barrier, inc=1, device_id=peer, device_id_type=pl.DeviceIdType.MESH)

    for copy in small:
        copy.wait()

    row = lax.broadcasted_iota(jnp.int32, (nodes, nodes), 0)
    column = lax.broadcasted_iota(jnp.int32, (nodes, nodes), 1)
    tile_count, listed = tile_ref.shape
    tile = nodes // tile_count
    column_tile = column // tile
    in_list = jnp.zeros((nodes, nodes), jnp.int32)
    for t in range(tile_count):
        hit = jnp.zeros((nodes, nodes), jnp.int32)
        for entry in range(listed):
            hit = jnp.where(column_tile == tile_ref[t, entry], 1, hit)
        in_list = jnp.where(row // tile == t, hit, in_list)
    row_graph = jnp.zeros((nodes, nodes), jnp.int32)
    column_graph = jnp.zeros((nodes, nodes), jnp.int32)
    end = 0
    for g in range(count_ref.shape[1]):
        end = end + count_ref[0, g]
        row_graph = row_graph + jnp.where(row >= end, 1, 0)
        column_graph = column_graph + jnp.where(column >= end, 1, 0)
    allowed_int = jnp.where((column <= row) & (row_graph == column_graph), in_list, 0)
    allowed = jnp.concatenate([allowed_int, allowed_int], axis=0) > 0
    low_lanes = lax.broadcasted_iota(jnp.int32, (nodes, LANES), 1) < HEAD

    own_rows = pl.ds(pl.multiple_of(x * nodes, nodes), nodes)
    other_rows = pl.ds(pl.multiple_of(other_x * nodes, nodes), nodes)

    squares = jnp.zeros((nodes, LANES), jnp.float32)
    piece_lanes = half // CHUNKS
    for pair in range(half // LANES):
        lanes = slice(pair * LANES, (pair + 1) * LANES)
        attended = pair_attention(
            query_ref[:, lanes], key_ref[:, lanes], value_ref[:, lanes], allowed, low_lanes
        )
        part = residual_ref[:, lanes].astype(jnp.float32) + attended
        stream[:, lanes] = part
        squares = squares + part * part
        chunk, offset = pair * LANES // piece_lanes, pair * LANES % piece_lanes
        gathered[z, core, x, chunk, :nodes, offset : offset + LANES] = (
            part * gain_ref[:, lanes]
        ).astype(jnp.bfloat16)

    item = lax.broadcasted_iota(jnp.int32, (AUX, nodes), 0)
    total = jnp.sum(squares.T, axis=0, keepdims=True)
    extra = jnp.where(item // 2 == rows_z, total, 0.0)
    for k in range(TOPK):
        gate = codes_ref[k : k + 1, :].astype(jnp.float32) / 65536.0
        extra = extra + jnp.where(item // 2 == ids_ref[k : k + 1, :], gate, 0.0)
    coarse = extra.astype(jnp.bfloat16).astype(jnp.float32)
    extra = jnp.where(item % 2 == 0, coarse, extra - coarse).astype(jnp.bfloat16)
    gathered[z, core, x, 0, nodes:, :LANES] = extra
    gathered[z, core, x, 0, nodes:, LANES:] = jnp.zeros((AUX, piece_lanes - LANES), jnp.bfloat16)

    def remote(src, dst, sent, received, device):
        return pltpu.make_async_remote_copy(
            src_ref=src,
            dst_ref=dst,
            send_sem=sent,
            recv_sem=received,
            device_id=device,
            device_id_type=pl.DeviceIdType.MESH,
        )

    def piece(zz, feature_half, xx, kind, step, chunk, device):
        ref = gathered.at[zz, feature_half, xx, chunk, pl.ds(0, nodes if chunk else nodes + AUX)]
        return remote(
            ref,
            ref,
            send_sem.at[kind, step, chunk],
            piece_sem.at[zz, feature_half, xx, chunk],
            device,
        )

    started = []

    def start(copy, condition=None):
        if condition is None:
            copy.start()
        else:
            pl.when(condition)(lambda: copy.start())
        started.append((copy, condition))

    def spread(step, chunk):
        zz = z_order[step]
        if step:
            piece(zz, core, x, 0, step, chunk, to_z[step]).wait_recv()
            start(piece(zz, core, x, 0, step, chunk, to_below), (zz > z) & (z > 0))
            start(piece(zz, core, x, 7, step, chunk, to_above), (zz < z) & (z < rows_z - 1))
        else:
            start(piece(zz, core, x, 0, 0, chunk, to_below), z > 0)
            start(piece(zz, core, x, 7, 0, chunk, to_above), z < rows_z - 1)
        start(piece(zz, core, x, 1, step, chunk, to_x))
        start(piece(zz, core, x, 2, step, chunk, to_core))

    def spread_other(step, chunk):
        zz = z_order[step]
        piece(zz, core, other_x, 1, step, chunk, to_x).wait_recv()
        start(piece(zz, core, other_x, 3, step, chunk, to_core))

    def copy_a(step):
        return remote(
            a_out.at[step], a_in.at[step], send_sem.at[4, step, 0], a_sem.at[step], to_core
        )

    def half_rows(part):
        return pl.ds(part * (nodes // 2), nodes // 2)

    def copy_b(step, part):
        rows = half_rows(part)
        return remote(
            b_out.at[step, rows],
            b_in.at[step, rows],
            send_sem.at[5, step, part],
            b_sem.at[step, part],
            to_x,
        )

    def copy_c(step, part, source):
        rows = half_rows(part)
        return remote(
            c_out.at[step, rows],
            c_in.at[source, rows],
            send_sem.at[6, step, part],
            c_sem.at[source, part],
            to_z[step],
        )

    own_lanes = pl.ds(pl.multiple_of(core * half, half), half)
    other_lanes = pl.ds(pl.multiple_of(other_core * half, half), half)

    def compute(step, between):
        zz = z_order[step]
        for chunk in range(CHUNKS):
            piece(zz, other_core, x, 2, step, chunk, to_core).wait_recv()
            piece(zz, other_core, other_x, 3, step, chunk, to_core).wait_recv()
        item = lax.broadcasted_iota(jnp.int32, (AUX, LANES), 0) // 2
        pick_square = jnp.where(item == rows_z, 1.0, 0.0).astype(jnp.bfloat16)
        pick_gate = jnp.where(item == z, 1.0, 0.0).astype(jnp.bfloat16)

        def column_of(feature_half, pick):
            return jnp.concatenate(
                [
                    lax.dot_general(
                        gathered[zz, feature_half, xx, 0, nodes:, :LANES],
                        pick,
                        (((0,), (0,)), ((), ())),
                        preferred_element_type=jnp.float32,
                    )[:, :1]
                    for xx in range(2)
                ],
                axis=0,
            )

        def rows_of(feature_half):
            return jnp.concatenate(
                [
                    jnp.concatenate(
                        [gathered[zz, feature_half, xx, chunk, :nodes] for chunk in range(CHUNKS)],
                        axis=1,
                    )
                    for xx in range(2)
                ],
                axis=0,
            )

        square = column_of(0, pick_square) + column_of(1, pick_square)
        scale = lax.rsqrt(square / width + epsilon)
        gate = column_of(0, pick_gate)
        chunk = half

        @pl.loop(0, ff // chunk)
        def _(j):
            lanes = pl.ds(pl.multiple_of(j * chunk, chunk), chunk)
            pre = jnp.dot(
                rows_of(0), w_up[:half, lanes], preferred_element_type=jnp.float32
            ) + jnp.dot(
                rows_of(1), w_up[half:, lanes], preferred_element_type=jnp.float32
            )
            hidden[:, lanes] = jax.nn.gelu(pre * scale).astype(jnp.bfloat16)

        between()
        sent = jnp.dot(hidden[...], w_down[:, other_lanes], preferred_element_type=jnp.float32)
        a_out[step] = (sent * gate).astype(jnp.bfloat16)
        start(copy_a(step))
        stays = jnp.dot(hidden[...], w_down[:, own_lanes], preferred_element_type=jnp.float32)
        kept[step] = stays * gate

    def add_cores(step):
        copy_a(step).wait_recv()
        b_out[step] = (
            kept[step, other_rows] + a_in[step, other_rows].astype(jnp.float32)
        ).astype(jnp.bfloat16)
        for part in range(2):
            start(copy_b(step, part))

    def add_columns(step):
        for part in range(2):
            copy_b(step, part).wait_recv()
            first = pl.multiple_of(x * nodes + part * (nodes // 2), nodes // 2)
            rows = pl.ds(first, nodes // 2)
            total = (
                kept[step, rows]
                + a_in[step, rows].astype(jnp.float32)
                + b_in[step, half_rows(part)].astype(jnp.float32)
            )
            if step:
                c_out[step, half_rows(part)] = total.astype(jnp.bfloat16)
                start(copy_c(step, part, z))
            else:
                stream[half_rows(part)] += total

    pl.semaphore_wait(barrier, len(peers))
    for chunk in range(CHUNKS):
        spread(0, chunk)
    for chunk in range(CHUNKS):
        spread(1, chunk)
        spread_other(0, chunk)
    load_up.wait()
    load_down.wait()
    for step in range(rows_z):

        def between(step=step):
            if step + 2 < rows_z:
                spread(step + 2, 0)
            if step == rows_z - 1:
                add_columns(step - 2)

        compute(step, between)
        if step + 2 < rows_z:
            for chunk in range(1, CHUNKS):
                spread(step + 2, chunk)
        if step + 1 < rows_z:
            for chunk in range(CHUNKS):
                spread_other(step + 1, chunk)
        if step >= 1:
            add_cores(step)
    add_columns(2)
    add_columns(3)
    add_cores(0)
    add_columns(0)

    result = stream[...]
    for step in range(1, rows_z):
        zz = z_order[step]
        for part in range(2):
            copy_c(step, part, zz).wait_recv()
        result = result + c_in[zz].astype(jnp.float32)
    out_ref[...] = result.astype(jnp.bfloat16)
    for copy, condition in started:
        if condition is None:
            copy.wait_send()
        else:
            pl.when(condition)(lambda copy=copy: copy.wait_send())


def fused_device(
    residual,
    queries,
    keys,
    values,
    tile_lists,
    node_counts,
    norm_gain,
    expert_ids,
    gate_codes,
    up_weight,
    down_weight,
):
    nodes, half = residual.shape
    ff = up_weight.shape[2]
    rows_z = lax.axis_size("dev") // 2
    bf16, f32 = jnp.bfloat16, jnp.float32
    hbm = pl.BlockSpec(memory_space=pl.ANY)
    return pl.pallas_call(
        functools.partial(layer_kernel, rows_z),
        out_shape=jax.ShapeDtypeStruct((nodes, half), bf16),
        in_specs=[hbm] * 11,
        out_specs=pl.BlockSpec(memory_space=pltpu.VMEM),
        scratch_shapes=[
            pltpu.SMEM(tile_lists.shape, jnp.int32),
            pltpu.SMEM(node_counts.shape, jnp.int32),
            pltpu.VMEM((nodes, half), bf16),
            pltpu.VMEM((nodes, half), bf16),
            pltpu.VMEM((nodes, half), bf16),
            pltpu.VMEM((nodes, half), bf16),
            pltpu.VMEM((1, half), f32),
            pltpu.VMEM((TOPK, nodes), jnp.int32),
            pltpu.VMEM((TOPK, nodes), jnp.int32),
            pltpu.VMEM((rows_z, 2, 2, CHUNKS, nodes + AUX, half // CHUNKS), bf16),
            pltpu.VMEM((nodes, half), f32),
            pltpu.VMEM(up_weight.shape[1:], bf16),
            pltpu.VMEM(down_weight.shape[1:], bf16),
            pltpu.VMEM((2 * nodes, ff), bf16),
            pltpu.VMEM((rows_z, 2 * nodes, half), f32),
            pltpu.VMEM((rows_z, 2 * nodes, half), bf16),
            pltpu.VMEM((rows_z, 2 * nodes, half), bf16),
            pltpu.VMEM((rows_z, nodes, half), bf16),
            pltpu.VMEM((rows_z, nodes, half), bf16),
            pltpu.VMEM((rows_z, nodes, half), bf16),
            pltpu.VMEM((rows_z, nodes, half), bf16),
            pltpu.SemaphoreType.DMA((11,)),
            pltpu.SemaphoreType.DMA((8, rows_z, CHUNKS)),
            pltpu.SemaphoreType.DMA((rows_z, 2, 2, CHUNKS)),
            pltpu.SemaphoreType.DMA((rows_z,)),
            pltpu.SemaphoreType.DMA((rows_z, 2)),
            pltpu.SemaphoreType.DMA((rows_z, 2)),
        ],
        compiler_params=pltpu.CompilerParams(
            collective_id=0, has_side_effects=True, vmem_limit_bytes=63 * 1024 * 1024
        ),
    )(
        tile_lists,
        node_counts,
        residual,
        queries,
        keys,
        values,
        norm_gain.reshape(1, half),
        expert_ids.T,
        gate_codes.T,
        up_weight,
        down_weight,
    )


def gathers_all(devices, nodes):
    experts = devices // 2
    capacity = 8 * nodes // devices
    return capacity >= nodes and 4 <= experts < 8


def layer(residual, *others):
    if gathers_all(lax.axis_size("dev"), residual.shape[0]):
        return fused_device(residual, *others)
    return per_device(residual, *others)


def solution(mesh):
    in_specs = (
        P(("groups", "dev"), "tp"),
        P(("groups", "dev"), "tp"),
        P(("groups", "dev"), "tp"),
        P(("groups", "dev"), "tp"),
        P(("groups", "dev"), None),
        P(("groups", "dev"), None),
        P("tp"),
        P(("groups", "dev"), None),
        P(("groups", "dev"), None),
        P("dev", None, "tp"),
        P("dev", "tp", None),
    )
    out_specs = P(("groups", "dev"), "tp")
    return jax.shard_map(
        layer, mesh=mesh, in_specs=in_specs, out_specs=out_specs, check_vma=False
    )
```

```python
import functools

import jax
import jax.numpy as jnp
from jax import lax
from jax.experimental import pallas as pl
from jax.experimental.pallas import tpu as pltpu
from jax.sharding import PartitionSpec as P

D = 1024
HEAD = 64
TOPK = 2


epsilon = 1e-06


def from_partner(value, axis, bit):
    return lax.ppermute(value, axis, [(i, i ^ 1 << bit) for i in range(lax.axis_size(axis))])


def cone_mask(tile_lists, node_counts, node_total):
    tile_count = tile_lists.shape[0]
    tile_size = node_total // tile_count
    tile_ids = jnp.arange(tile_count, dtype=jnp.int32)
    tile_ok = jnp.any(tile_lists[:, :, None] == tile_ids[None, None, :], axis=1)
    node_ok = jnp.broadcast_to(
        tile_ok[:, None, :, None], (tile_count, tile_size, tile_count, tile_size)
    ).reshape(node_total, node_total)
    nodes = jnp.arange(node_total, dtype=jnp.int32)
    graph_ends = jnp.cumsum(node_counts)
    graph_of = jnp.sum((nodes[:, None] >= graph_ends[None, :]).astype(jnp.int32), axis=1)
    same_graph = graph_of[:, None] == graph_of[None, :]
    return node_ok & same_graph & (nodes[None, :] <= nodes[:, None])


def cone_attention(queries, keys, values, allowed):
    node_total, width = queries.shape
    head_count = width // HEAD
    query_heads = queries.reshape(node_total, head_count, HEAD)
    key_heads = keys.reshape(node_total, head_count, HEAD)
    value_heads = values.reshape(node_total, head_count, HEAD)
    scores = jnp.einsum(
        "qhd,khd->hqk", query_heads, key_heads, preferred_element_type=jnp.float32
    ) * HEAD ** (-0.5)
    scores = jnp.where(allowed[None], scores, -1e30)
    highest = jnp.max(scores, axis=2, keepdims=True)
    weights = jnp.where(allowed[None], jnp.exp(scores - highest), 0.0)
    denominator = jnp.sum(weights, axis=2, keepdims=True)
    probs = (weights / denominator).astype(jnp.bfloat16)
    attended = jnp.einsum("hqk,khd->qhd", probs, value_heads, preferred_element_type=jnp.float32)
    return attended.reshape(node_total, width)


def slots_of(flat_ids, expert_count):
    onehot = (flat_ids[..., None] == jnp.arange(expert_count, dtype=jnp.int32)).astype(jnp.int32)
    before = jnp.cumsum(onehot, axis=-2) - onehot
    return jnp.sum(before * onehot, axis=-1)


def per_device(
    residual,
    queries,
    keys,
    values,
    tile_lists,
    node_counts,
    norm_gain,
    expert_ids,
    gate_codes,
    up_weight,
    down_weight,
):
    node_total = residual.shape[0]
    half_width = residual.shape[1]
    quarter = half_width // 2
    devices = lax.axis_size("dev")
    experts = devices // 2
    capacity = 8 * node_total // devices
    parity = lax.axis_index("dev") % 2
    allowed = cone_mask(tile_lists, node_counts[0], node_total)
    stream = residual.astype(jnp.float32) + cone_attention(queries, keys, values, allowed)
    squares = lax.psum(jnp.sum(stream * stream, axis=1), "tp")
    normed = (stream * lax.rsqrt(squares / D + epsilon)[:, None] * norm_gain).astype(jnp.bfloat16)
    flat_ids = expert_ids.reshape(-1)
    slot_index = slots_of(flat_ids, experts)
    row_ids = jnp.arange(experts * capacity, dtype=jnp.int32)
    hits = (flat_ids[None, :] == (row_ids // capacity)[:, None]) & (
        slot_index[None, :] == (row_ids % capacity)[:, None]
    )
    dispatch = jnp.sum(
        hits.reshape(experts * capacity, node_total, TOPK).astype(jnp.int32), axis=2
    ).astype(jnp.bfloat16)
    packed = jnp.dot(dispatch, normed, preferred_element_type=jnp.float32).astype(jnp.bfloat16)
    outgoing = jnp.broadcast_to(
        packed.reshape(experts, 1, capacity, half_width), (experts, 2, capacity, half_width)
    ).reshape(devices * capacity, half_width)
    arrived = lax.all_to_all(outgoing, "dev", split_axis=0, concat_axis=0, tiled=True)
    w_up = up_weight[0]
    w_down = down_weight[0]
    up_whole, down_whole = (
        lax.all_gather(w_up, "tp", axis=1, tiled=True),
        lax.all_gather(w_down, "tp", axis=0, tiled=True),
    )
    served = lax.all_to_all(arrived, "tp", split_axis=0, concat_axis=1, tiled=True)
    hidden = jax.nn.gelu(jnp.dot(served, up_whole, preferred_element_type=jnp.float32)).astype(
        jnp.bfloat16
    )
    served_out = jnp.dot(hidden, down_whole, preferred_element_type=jnp.float32)
    summed_half = lax.all_to_all(served_out, "tp", split_axis=1, concat_axis=0, tiled=True)
    outgoing_share = lax.dynamic_slice_in_dim(summed_half, (1 - parity) * quarter, quarter, 1)
    kept_share = lax.dynamic_slice_in_dim(summed_half, parity * quarter, quarter, 1)
    finished = (
        kept_share
        + from_partner(outgoing_share.astype(jnp.bfloat16), "dev", 0).astype(outgoing_share.dtype)
    ).astype(jnp.bfloat16)
    returned = lax.all_to_all(finished, "dev", split_axis=0, concat_axis=1, tiled=True)
    returned = returned.reshape(capacity * experts, half_width)
    node_slots = slot_index.reshape(node_total, TOPK)
    gates = gate_codes.astype(jnp.float32) / 65536.0
    back_rows = jnp.arange(capacity * experts, dtype=jnp.int32)
    added = jnp.zeros((node_total, half_width), jnp.float32)
    for which in range(TOPK):
        picker = (
            (expert_ids[:, which][None, :] == (back_rows % experts)[:, None])
            & (node_slots[:, which][None, :] == (back_rows // experts)[:, None])
        ).astype(jnp.bfloat16)
        fetched = lax.dot_general(
            picker, returned, (((0,), (0,)), ((), ())), preferred_element_type=jnp.float32
        )
        added = added + gates[:, which : which + 1] * fetched
    return (stream + added).astype(jnp.bfloat16)


AUX = 16
CHUNKS = 2
LANES = 128


def pair_attention(query_pair, key_pair, value_pair, allowed, low_lanes):
    nodes = query_pair.shape[0]
    zero = jnp.zeros_like(query_pair)
    stacked = jnp.concatenate(
        [jnp.where(low_lanes, query_pair, zero), jnp.where(low_lanes, zero, query_pair)], axis=0
    )
    scores = lax.dot_general(
        stacked, key_pair, (((1,), (1,)), ((), ())), preferred_element_type=jnp.float32
    ) * HEAD ** (-0.5)
    scores = jnp.where(allowed, scores, -1e30)
    highest = jnp.max(scores, axis=1, keepdims=True)
    weights = jnp.where(allowed, jnp.exp(scores - highest), 0.0)
    denominator = jnp.sum(weights, axis=1, keepdims=True)
    probs = (weights / denominator).astype(jnp.bfloat16)
    both = jnp.dot(probs, value_pair, preferred_element_type=jnp.float32)
    return jnp.where(low_lanes, both[:nodes], both[nodes:])


def layer_kernel(
    rows_z,
    tile_hbm,
    count_hbm,
    residual_hbm,
    query_hbm,
    key_hbm,
    value_hbm,
    gain_hbm,
    ids_hbm,
    codes_hbm,
    up_ref,
    down_ref,
    out_ref,
    tile_ref,
    count_ref,
    residual_ref,
    query_ref,
    key_ref,
    value_ref,
    gain_ref,
    ids_ref,
    codes_ref,
    gathered,
    stream,
    w_up,
    w_down,
    hidden,
    kept,
    a_out,
    a_in,
    b_out,
    b_in,
    c_out,
    c_in,
    w_sem,
    send_sem,
    piece_sem,
    a_sem,
    b_sem,
    c_sem,
):
    nodes, half = residual_ref.shape
    ff = up_ref.shape[2]
    width = 2 * half
    dev = lax.axis_index("dev")
    core = lax.axis_index("tp")
    z, x = dev // 2, dev % 2
    other_core = 1 - core
    other_x = 1 - x

    orders = []
    for place in range(rows_z):
        order = [place]
        for distance in range(1, rows_z):
            order += [r for r in (place + distance, place - distance) if 0 <= r < rows_z]
        orders.append(order)

    def z_of(step):
        found = orders[0][step]
        for place in range(1, rows_z):
            found = jnp.where(z == place, orders[place][step], found)
        return found

    z_order = [z] + [z_of(step) for step in range(1, rows_z)]

    small = []
    for hbm, near in (
        (tile_hbm, tile_ref),
        (count_hbm, count_ref),
        (query_hbm, query_ref),
        (key_hbm, key_ref),
        (value_hbm, value_ref),
        (residual_hbm, residual_ref),
        (gain_hbm, gain_ref),
        (ids_hbm, ids_ref),
        (codes_hbm, codes_ref),
    ):
        copy = pltpu.make_async_copy(hbm, near, w_sem.at[2 + len(small)])
        copy.start()
        small.append(copy)
    load_up = pltpu.make_async_copy(up_ref.at[0], w_up, w_sem.at[0])
    load_down = pltpu.make_async_copy(down_ref.at[0], w_down, w_sem.at[1])
    load_up.start()
    load_down.start()

    barrier = pltpu.get_barrier_semaphore()
    to_core = {"tp": other_core}
    to_x = {"dev": 2 * z + other_x}
    to_z = [{"dev": 2 * zz + x} for zz in z_order]
    to_above, to_below = {"dev": dev + 2}, {"dev": dev - 2}
    peers = [to_core, to_x] + to_z[1:]
    for peer in peers:
        pl.semaphore_signal(barrier, inc=1, device_id=peer, device_id_type=pl.DeviceIdType.MESH)

    for copy in small:
        copy.wait()

    row = lax.broadcasted_iota(jnp.int32, (nodes, nodes), 0)
    column = lax.broadcasted_iota(jnp.int32, (nodes, nodes), 1)
    tile_count, listed = tile_ref.shape
    tile = nodes // tile_count
    column_tile = column // tile
    in_list = jnp.zeros((nodes, nodes), jnp.int32)
    for t in range(tile_count):
        hit = jnp.zeros((nodes, nodes), jnp.int32)
        for entry in range(listed):
            hit = jnp.where(column_tile == tile_ref[t, entry], 1, hit)
        in_list = jnp.where(row // tile == t, hit, in_list)
    row_graph = jnp.zeros((nodes, nodes), jnp.int32)
    column_graph = jnp.zeros((nodes, nodes), jnp.int32)
    end = 0
    for g in range(count_ref.shape[1]):
        end = end + count_ref[0, g]
        row_graph = row_graph + jnp.where(row >= end, 1, 0)
        column_graph = column_graph + jnp.where(column >= end, 1, 0)
    allowed_int = jnp.where((column <= row) & (row_graph == column_graph), in_list, 0)
    allowed = jnp.concatenate([allowed_int, allowed_int], axis=0) > 0
    low_lanes = lax.broadcasted_iota(jnp.int32, (nodes, LANES), 1) < HEAD

    own_rows = pl.ds(pl.multiple_of(x * nodes, nodes), nodes)
    other_rows = pl.ds(pl.multiple_of(other_x * nodes, nodes), nodes)

    squares = jnp.zeros((nodes, LANES), jnp.float32)
    piece_lanes = half // CHUNKS
    for pair in range(half // LANES):
        lanes = slice(pair * LANES, (pair + 1) * LANES)
        attended = pair_attention(
            query_ref[:, lanes], key_ref[:, lanes], value_ref[:, lanes], allowed, low_lanes
        )
        part = residual_ref[:, lanes].astype(jnp.float32) + attended
        stream[:, lanes] = part
        squares = squares + part * part
        chunk, offset = pair * LANES // piece_lanes, pair * LANES % piece_lanes
        gathered[z, core, x, chunk, :nodes, offset : offset + LANES] = (
            part * gain_ref[:, lanes]
        ).astype(jnp.bfloat16)

    item = lax.broadcasted_iota(jnp.int32, (AUX, nodes), 0)
    total = jnp.sum(squares.T, axis=0, keepdims=True)
    extra = jnp.where(item // 2 == rows_z, total, 0.0)
    for k in range(TOPK):
        gate = codes_ref[k : k + 1, :].astype(jnp.float32) / 65536.0
        extra = extra + jnp.where(item // 2 == ids_ref[k : k + 1, :], gate, 0.0)
    coarse = extra.astype(jnp.bfloat16).astype(jnp.float32)
    extra = jnp.where(item % 2 == 0, coarse, extra - coarse).astype(jnp.bfloat16)
    gathered[z, core, x, 0, nodes:, :LANES] = extra
    gathered[z, core, x, 0, nodes:, LANES:] = jnp.zeros((AUX, piece_lanes - LANES), jnp.bfloat16)

    def remote(src, dst, sent, received, device):
        return pltpu.make_async_remote_copy(
            src_ref=src,
            dst_ref=dst,
            send_sem=sent,
            recv_sem=received,
            device_id=device,
            device_id_type=pl.DeviceIdType.MESH,
        )

    def piece(zz, feature_half, xx, kind, step, chunk, device):
        ref = gathered.at[zz, feature_half, xx, chunk, pl.ds(0, nodes if chunk else nodes + AUX)]
        return remote(
            ref,
            ref,
            send_sem.at[kind, step, chunk],
            piece_sem.at[zz, feature_half, xx, chunk],
            device,
        )

    started = []

    def start(copy, condition=None):
        if condition is None:
            copy.start()
        else:
            pl.when(condition)(lambda: copy.start())
        started.append((copy, condition))

    def spread(step, chunk):
        zz = z_order[step]
        if step:
            piece(zz, core, x, 0, step, chunk, to_z[step]).wait_recv()
            start(piece(zz, core, x, 0, step, chunk, to_below), (zz > z) & (z > 0))
            start(piece(zz, core, x, 7, step, chunk, to_above), (zz < z) & (z < rows_z - 1))
        else:
            start(piece(zz, core, x, 0, 0, chunk, to_below), z > 0)
            start(piece(zz, core, x, 7, 0, chunk, to_above), z < rows_z - 1)
        start(piece(zz, core, x, 1, step, chunk, to_x))
        start(piece(zz, core, x, 2, step, chunk, to_core))

    def spread_other(step, chunk):
        zz = z_order[step]
        piece(zz, core, other_x, 1, step, chunk, to_x).wait_recv()
        start(piece(zz, core, other_x, 3, step, chunk, to_core))

    def copy_a(step, part):
        rows = own_rows if part else other_rows
        return remote(
            a_out.at[step, rows],
            a_in.at[step, rows],
            send_sem.at[4, step, part],
            a_sem.at[step, part],
            to_core,
        )

    def half_rows(part):
        return pl.ds(part * (nodes // 2), nodes // 2)

    def copy_b(step, part):
        rows = half_rows(part)
        return remote(
            b_out.at[step, rows],
            b_in.at[step, rows],
            send_sem.at[5, step, part],
            b_sem.at[step, part],
            to_x,
        )

    def copy_c(step, part, source):
        rows = half_rows(part)
        return remote(
            c_out.at[step, rows],
            c_in.at[source, rows],
            send_sem.at[6, step, part],
            c_sem.at[source, part],
            to_z[step],
        )

    own_lanes = pl.ds(pl.multiple_of(core * half, half), half)
    other_lanes = pl.ds(pl.multiple_of(other_core * half, half), half)

    def compute(step, between):
        zz = z_order[step]
        for chunk in range(CHUNKS):
            piece(zz, other_core, x, 2, step, chunk, to_core).wait_recv()
            piece(zz, other_core, other_x, 3, step, chunk, to_core).wait_recv()
        item = lax.broadcasted_iota(jnp.int32, (AUX, LANES), 0) // 2
        pick_square = jnp.where(item == rows_z, 1.0, 0.0).astype(jnp.bfloat16)
        pick_gate = jnp.where(item == z, 1.0, 0.0).astype(jnp.bfloat16)

        def column_of(feature_half, pick):
            return jnp.concatenate(
                [
                    lax.dot_general(
                        gathered[zz, feature_half, xx, 0, nodes:, :LANES],
                        pick,
                        (((0,), (0,)), ((), ())),
                        preferred_element_type=jnp.float32,
                    )[:, :1]
                    for xx in range(2)
                ],
                axis=0,
            )

        def rows_of(feature_half):
            return jnp.concatenate(
                [
                    jnp.concatenate(
                        [gathered[zz, feature_half, xx, chunk, :nodes] for chunk in range(CHUNKS)],
                        axis=1,
                    )
                    for xx in range(2)
                ],
                axis=0,
            )

        square = column_of(0, pick_square) + column_of(1, pick_square)
        scale = lax.rsqrt(square / width + epsilon)
        gate = column_of(0, pick_gate)
        chunk = half

        @pl.loop(0, ff // chunk)
        def _(j):
            lanes = pl.ds(pl.multiple_of(j * chunk, chunk), chunk)
            pre = jnp.dot(
                rows_of(0), w_up[:half, lanes], preferred_element_type=jnp.float32
            ) + jnp.dot(
                rows_of(1), w_up[half:, lanes], preferred_element_type=jnp.float32
            )
            hidden[:, lanes] = jax.nn.gelu(pre * scale).astype(jnp.bfloat16)

        between()
        sent = jnp.dot(hidden[...], w_down[:, other_lanes], preferred_element_type=jnp.float32)
        a_out[step] = (sent * gate).astype(jnp.bfloat16)
        for part in range(2):
            start(copy_a(step, part))
        stays = jnp.dot(hidden[...], w_down[:, own_lanes], preferred_element_type=jnp.float32)
        kept[step] = stays * gate

    def add_cores(step):
        copy_a(step, 0).wait_recv()
        for part in range(2):
            first = pl.multiple_of(other_x * nodes + part * (nodes // 2), nodes // 2)
            rows = pl.ds(first, nodes // 2)
            b_out[step, half_rows(part)] = (
                kept[step, rows] + a_in[step, rows].astype(jnp.float32)
            ).astype(jnp.bfloat16)
            start(copy_b(step, part))

    def add_columns(step):
        copy_a(step, 1).wait_recv()
        for part in range(2):
            copy_b(step, part).wait_recv()
            first = pl.multiple_of(x * nodes + part * (nodes // 2), nodes // 2)
            rows = pl.ds(first, nodes // 2)
            total = (
                kept[step, rows]
                + a_in[step, rows].astype(jnp.float32)
                + b_in[step, half_rows(part)].astype(jnp.float32)
            )
            if step:
                c_out[step, half_rows(part)] = total.astype(jnp.bfloat16)
                start(copy_c(step, part, z))
            else:
                stream[half_rows(part)] += total

    pl.semaphore_wait(barrier, len(peers))
    for chunk in range(CHUNKS):
        spread(0, chunk)
    for chunk in range(CHUNKS):
        spread(1, chunk)
        spread_other(0, chunk)
    load_up.wait()
    load_down.wait()
    for step in range(rows_z):

        def between(step=step):
            if step + 2 < rows_z:
                spread(step + 2, 0)
            if step == rows_z - 1:
                add_columns(step - 2)

        compute(step, between)
        if step + 2 < rows_z:
            for chunk in range(1, CHUNKS):
                spread(step + 2, chunk)
        if step + 1 < rows_z:
            for chunk in range(CHUNKS):
                spread_other(step + 1, chunk)
        if step >= 1:
            add_cores(step)
    add_columns(2)
    add_columns(3)
    add_cores(0)
    add_columns(0)

    result = stream[...]
    for step in range(1, rows_z):
        zz = z_order[step]
        for part in range(2):
            copy_c(step, part, zz).wait_recv()
        result = result + c_in[zz].astype(jnp.float32)
    out_ref[...] = result.astype(jnp.bfloat16)
    for copy, condition in started:
        if condition is None:
            copy.wait_send()
        else:
            pl.when(condition)(lambda copy=copy: copy.wait_send())


def fused_device(
    residual,
    queries,
    keys,
    values,
    tile_lists,
    node_counts,
    norm_gain,
    expert_ids,
    gate_codes,
    up_weight,
    down_weight,
):
    nodes, half = residual.shape
    ff = up_weight.shape[2]
    rows_z = lax.axis_size("dev") // 2
    bf16, f32 = jnp.bfloat16, jnp.float32
    hbm = pl.BlockSpec(memory_space=pl.ANY)
    return pl.pallas_call(
        functools.partial(layer_kernel, rows_z),
        out_shape=jax.ShapeDtypeStruct((nodes, half), bf16),
        in_specs=[hbm] * 11,
        out_specs=pl.BlockSpec(memory_space=pltpu.VMEM),
        scratch_shapes=[
            pltpu.SMEM(tile_lists.shape, jnp.int32),
            pltpu.SMEM(node_counts.shape, jnp.int32),
            pltpu.VMEM((nodes, half), bf16),
            pltpu.VMEM((nodes, half), bf16),
            pltpu.VMEM((nodes, half), bf16),
            pltpu.VMEM((nodes, half), bf16),
            pltpu.VMEM((1, half), f32),
            pltpu.VMEM((TOPK, nodes), jnp.int32),
            pltpu.VMEM((TOPK, nodes), jnp.int32),
            pltpu.VMEM((rows_z, 2, 2, CHUNKS, nodes + AUX, half // CHUNKS), bf16),
            pltpu.VMEM((nodes, half), f32),
            pltpu.VMEM(up_weight.shape[1:], bf16),
            pltpu.VMEM(down_weight.shape[1:], bf16),
            pltpu.VMEM((2 * nodes, ff), bf16),
            pltpu.VMEM((rows_z, 2 * nodes, half), f32),
            pltpu.VMEM((rows_z, 2 * nodes, half), bf16),
            pltpu.VMEM((rows_z, 2 * nodes, half), bf16),
            pltpu.VMEM((rows_z, nodes, half), bf16),
            pltpu.VMEM((rows_z, nodes, half), bf16),
            pltpu.VMEM((rows_z, nodes, half), bf16),
            pltpu.VMEM((rows_z, nodes, half), bf16),
            pltpu.SemaphoreType.DMA((11,)),
            pltpu.SemaphoreType.DMA((8, rows_z, CHUNKS)),
            pltpu.SemaphoreType.DMA((rows_z, 2, 2, CHUNKS)),
            pltpu.SemaphoreType.DMA((rows_z, 2)),
            pltpu.SemaphoreType.DMA((rows_z, 2)),
            pltpu.SemaphoreType.DMA((rows_z, 2)),
        ],
        compiler_params=pltpu.CompilerParams(
            collective_id=0, has_side_effects=True, vmem_limit_bytes=63 * 1024 * 1024
        ),
    )(
        tile_lists,
        node_counts,
        residual,
        queries,
        keys,
        values,
        norm_gain.reshape(1, half),
        expert_ids.T,
        gate_codes.T,
        up_weight,
        down_weight,
    )


def gathers_all(devices, nodes):
    experts = devices // 2
    capacity = 8 * nodes // devices
    return capacity >= nodes and 4 <= experts < 8


def layer(residual, *others):
    if gathers_all(lax.axis_size("dev"), residual.shape[0]):
        return fused_device(residual, *others)
    return per_device(residual, *others)


def solution(mesh):
    in_specs = (
        P(("groups", "dev"), "tp"),
        P(("groups", "dev"), "tp"),
        P(("groups", "dev"), "tp"),
        P(("groups", "dev"), "tp"),
        P(("groups", "dev"), None),
        P(("groups", "dev"), None),
        P("tp"),
        P(("groups", "dev"), None),
        P(("groups", "dev"), None),
        P("dev", None, "tp"),
        P("dev", "tp", None),
    )
    out_specs = P(("groups", "dev"), "tp")
    return jax.shard_map(
        layer, mesh=mesh, in_specs=in_specs, out_specs=out_specs, check_vma=False
    )
```
